32 devices in a mesh: seq: 8 (over z, y), mp: 4 (over x, core).
Axes of the slice: x: 2, y: 2, z: 4, core: 2. Of those that a mesh axis runs over, the one named last changes fastest.
Arguments:
- tokens: bfloat16 [2304, 1536], P('seq'), may hold values from -6 to 6
- norm_gain: float32 [1536], replicated, may hold values from 0.5 to 1.5
- w_query: bfloat16 [1536, 1536], P(None, 'mp')
- w_key: bfloat16 [1536, 1536], P(None, 'mp')
- w_value: bfloat16 [1536, 1536], P(None, 'mp'), may hold values from -0.15625 to 0.15625
- w_out: bfloat16 [1536, 1536], P('mp'), may hold values from -0.15625 to 0.15625
- w_shorten: bfloat16 [13824, 1536], P('seq', 'mp'), may hold values from -0.0546875 to 0.0546875
- first_key: int32 [256], P('seq'), may hold values from 0 to 2295, as said below
- d_faces: bfloat16 [256, 1536], P('seq', 'mp'), may hold values from -6 to 6
Outputs:
- faces: bfloat16 [256, 1536], P('seq', 'mp')
- d_tokens: bfloat16 [2304, 1536], P('seq')
The draws below stay inside these ranges and needn't reach their ends.
Inputs may be any that keep to these rules, and one draw needn't show every extreme that they name: first_key is a multiple of 9, never above the position of its face's first token, never decreases from one face to the next, and equals that position at every face where a new mesh begins; face 0 and the last face begin meshes.
All inputs are finite; a program needn't handle non-finite values.
Results may differ from the reference program's by a relative error of at most 0.014.
Values may be sent and summed in bfloat16 or wider, within the bound.
A program may use at most 128 MiB of HBM per device.

```python
import jax
import jax.numpy as jnp
from jax import lax

HEADS = 24
HEAD = 64
D = 1536
WIN = 4096
T_DEV = 288
FACES = 256
TOKENS = 2304
HOPS = 7
N_SEQ = 8


def weight_pair(key):
    base = jax.random.normal(jax.random.fold_in(key, 7), (D, D), jnp.float32) * D ** (-0.5)
    other = jax.random.normal(jax.random.fold_in(key, 8), (D, D), jnp.float32) * D ** (-0.5)
    return (base, other)


def draw_w_query(key, part):
    base, other = weight_pair(key)
    return base.astype(jnp.bfloat16)


def draw_w_key(key, part):
    base, other = weight_pair(key)
    return other.astype(jnp.bfloat16)


def draw_first_key(key, part):
    flags = jax.random.randint(jax.random.fold_in(key, 3), (FACES,), 0, max(2, WIN // 12))
    index = jnp.arange(FACES, dtype=jnp.int32)
    begins = (flags == 0) | (index == 0) | (index == FACES - 1)
    starts = jnp.where(begins, index, 0)
    return (lax.cummax(starts, axis=0) * 9).astype(jnp.int32)


def block_scale(own_key, extent, pieces, least, high):
    factor_of, own = 1.0, jax.random.fold_in(own_key, 6)
    for position, shards_of in pieces:
        draws = jnp.exp(jax.random.uniform(jax.random.fold_in(own, position), (shards_of,), jnp.float32, least / len(pieces), high / len(pieces)))
        factor_of = factor_of * jnp.repeat(draws, extent[position] // shards_of).reshape([-1 if axis == position else 1 for axis in range(len(extent))])
    return factor_of


def bell_draw(key, dims, scale, most, cuts=(), held_as=jnp.bfloat16):
    values = scale * jax.random.normal(key, dims, jnp.float32)
    if cuts:
        values = values * block_scale(key, dims, cuts, -0.22, 0.18)
    return jnp.clip(values, -most, most).astype(held_as)


def setup_inputs(seed: int = 0) -> dict:
    key_list = jax.random.split(jax.random.key(seed), 10)
    tokens = bell_draw(key_list[0], (TOKENS, D), 1.0, 6.0, ((0, 8),))
    norm_gain = jnp.clip(1.0 + 0.1 * jax.random.normal(key_list[1], (D,), jnp.float32), 0.5, 1.5)
    w_query = draw_w_query(jax.random.fold_in(key_list[9], 71), 0)
    w_key = draw_w_key(jax.random.fold_in(key_list[9], 71), 0)
    w_value = bell_draw(key_list[4], (D, D), D ** -0.5, 0.15625, ((1, 4),))
    w_out = bell_draw(key_list[5], (D, D), D ** -0.5, 0.15625, ((0, 4),))
    w_shorten = bell_draw(key_list[6], (9 * D, D), (9 * D) ** -0.5, 0.0546875, ((0, 8), (1, 4)))
    first_key = draw_first_key(jax.random.fold_in(key_list[9], 71), 0)
    d_faces = bell_draw(key_list[8], (FACES, D), 1.0, 6.0, ((0, 8), (1, 4)))
    return dict(tokens=tokens, norm_gain=norm_gain, w_query=w_query, w_key=w_key, w_value=w_value, w_out=w_out, w_shorten=w_shorten, first_key=first_key, d_faces=d_faces)


def probabilities(query_blk, key_blk, pos_q, pos_k, lower_bound):
    scores = jnp.einsum('thd,khd->htk', query_blk.astype(jnp.float32), key_blk.astype(jnp.float32)) * HEAD ** (-0.5)
    allowed = (pos_k[None, :] >= lower_bound[:, None]) & (pos_k[None, :] <= pos_q[:, None]) & (pos_q[:, None] - pos_k[None, :] < WIN)
    scores = jnp.where(allowed[None], scores, -1e+30)
    row_top = lax.optimization_barrier(jnp.max(scores, axis=-1, keepdims=True))
    raised = jnp.exp(scores - row_top)
    return raised / lax.optimization_barrier(jnp.sum(raised, axis=-1, keepdims=True))

def reference(tokens, norm_gain, w_query, w_key, w_value, w_out, w_shorten, first_key, d_faces):
    x_float = tokens.astype(jnp.float32)
    scale_r = lax.rsqrt(lax.optimization_barrier(jnp.mean(x_float * x_float, axis=-1, keepdims=True)) + 1e-05)
    normed = (x_float * scale_r * norm_gain).astype(jnp.bfloat16)
    query = jnp.dot(normed, w_query, preferred_element_type=jnp.float32).astype(jnp.bfloat16)
    key = jnp.dot(normed, w_key, preferred_element_type=jnp.float32).astype(jnp.bfloat16)
    value = jnp.dot(normed, w_value, preferred_element_type=jnp.float32).astype(jnp.bfloat16)
    key_span = (HOPS + 1) * T_DEV
    prefix = HOPS * T_DEV
    bound_all = jnp.repeat(first_key, 9)
    key_pad = jnp.concatenate([jnp.zeros((prefix, D), jnp.bfloat16), key], axis=0)
    value_pad = jnp.concatenate([jnp.zeros((prefix, D), jnp.bfloat16), value], axis=0)

    def block_inputs(block_idx):
        first_row = (block_idx * T_DEV).astype(jnp.int32)
        query_blk = lax.dynamic_slice_in_dim(query, first_row, T_DEV, 0).reshape(T_DEV, HEADS, HEAD)
        key_blk = lax.dynamic_slice_in_dim(key_pad, first_row, key_span, 0).reshape(key_span, HEADS, HEAD)
        value_blk = lax.dynamic_slice_in_dim(value_pad, first_row, key_span, 0).reshape(key_span, HEADS, HEAD)
        pos_q = first_row + jnp.arange(T_DEV, dtype=jnp.int32)
        pos_k = first_row - prefix + jnp.arange(key_span, dtype=jnp.int32)
        lower_bound = lax.dynamic_slice_in_dim(bound_all, first_row, T_DEV, 0)
        return (query_blk, key_blk, value_blk, pos_q, pos_k, lower_bound)

    def forward_block(block_idx):
        query_blk, key_blk, value_blk, pos_q, pos_k, lower_bound = block_inputs(block_idx)
        probs = probabilities(query_blk, key_blk, pos_q, pos_k, lower_bound)
        outcome = jnp.einsum('htk,khd->thd', probs.astype(jnp.bfloat16).astype(jnp.float32), value_blk.astype(jnp.float32))
        return outcome.reshape(T_DEV, D).astype(jnp.bfloat16)
    blocks = jnp.arange(N_SEQ, dtype=jnp.int32)
    attended = lax.map(forward_block, blocks).reshape(TOKENS, D)
    mixed = (x_float + jnp.dot(attended, w_out, preferred_element_type=jnp.float32)).astype(jnp.bfloat16)
    faces = jnp.dot(mixed.reshape(FACES, 9 * D), w_shorten, preferred_element_type=jnp.float32).astype(jnp.bfloat16)
    d_mixed = jnp.dot(d_faces, w_shorten.T, preferred_element_type=jnp.float32).astype(jnp.bfloat16).reshape(TOKENS, D)
    d_attended = jnp.dot(d_mixed, w_out.T, preferred_element_type=jnp.float32).astype(jnp.bfloat16)

    def backward_step(block_idx, carry):
        d_query_all, d_key_pad, d_value_pad = carry
        query_blk, key_blk, value_blk, pos_q, pos_k, lower_bound = block_inputs(block_idx)
        probs = probabilities(query_blk, key_blk, pos_q, pos_k, lower_bound)
        first_row = (block_idx * T_DEV).astype(jnp.int32)
        d_att_blk = lax.dynamic_slice_in_dim(d_attended, first_row, T_DEV, 0).reshape(T_DEV, HEADS, HEAD).astype(jnp.float32)
        att_blk = lax.dynamic_slice_in_dim(attended, first_row, T_DEV, 0).reshape(T_DEV, HEADS, HEAD).astype(jnp.float32)
        d_probs = jnp.einsum('thd,khd->htk', d_att_blk, value_blk.astype(jnp.float32))
        row_delta = jnp.einsum('thd,thd->ht', d_att_blk, att_blk)
        d_scores = (probs * (d_probs - row_delta[:, :, None])).astype(jnp.bfloat16).astype(jnp.float32)
        d_query_blk = (jnp.einsum('htk,khd->thd', d_scores, key_blk.astype(jnp.float32)) * HEAD ** (-0.5)).astype(jnp.bfloat16)
        d_key_blk = jnp.einsum('htk,thd->khd', d_scores, query_blk.astype(jnp.float32)) * HEAD ** (-0.5)
        d_value_blk = jnp.einsum('htk,thd->khd', probs.astype(jnp.bfloat16).astype(jnp.float32), d_att_blk)
        zero_col = jnp.zeros((), jnp.int32)
        d_query_all = lax.dynamic_update_slice(d_query_all, d_query_blk.reshape(T_DEV, D), (first_row, zero_col))
        old_key = lax.dynamic_slice(d_key_pad, (first_row, zero_col), (key_span, D))
        d_key_pad = lax.dynamic_update_slice(d_key_pad, old_key + d_key_blk.reshape(key_span, D), (first_row, zero_col))
        old_value = lax.dynamic_slice(d_value_pad, (first_row, zero_col), (key_span, D))
        d_value_pad = lax.dynamic_update_slice(d_value_pad, old_value + d_value_blk.reshape(key_span, D), (first_row, zero_col))
        return (d_query_all, d_key_pad, d_value_pad)
    start_carry = (jnp.zeros((TOKENS, D), jnp.bfloat16), jnp.zeros((prefix + TOKENS, D), jnp.float32), jnp.zeros((prefix + TOKENS, D), jnp.float32))
    d_query, d_key_pad, d_value_pad = lax.fori_loop(0, N_SEQ, backward_step, start_carry)
    d_key = d_key_pad[prefix:].astype(jnp.bfloat16)
    d_value = d_value_pad[prefix:].astype(jnp.bfloat16)
    d_normed = jnp.dot(d_query, w_query.T, preferred_element_type=jnp.float32)
    d_normed = d_normed + jnp.dot(d_key, w_key.T, preferred_element_type=jnp.float32)
    d_normed = d_normed + jnp.dot(d_value, w_value.T, preferred_element_type=jnp.float32)
    inner_sum = lax.optimization_barrier(jnp.mean(d_normed * norm_gain * x_float, axis=-1, keepdims=True))
    d_tokens = d_mixed.astype(jnp.float32) + scale_r * norm_gain * d_normed - x_float * scale_r ** 3 * inner_sum
    return (faces, d_tokens.astype(jnp.bfloat16))
```

```python
import functools

import jax
import jax.numpy as jnp
from jax import lax
from jax.experimental import pallas as pl
from jax.experimental.pallas import tpu as pltpu
from jax.sharding import PartitionSpec as P

HEAD = 64
WIN = 4096
LANES = 2 * HEAD


def shifted(array, axis, by):
    size = lax.axis_size(axis)
    pairs = [(i, i + by) for i in range(size) if 0 <= i + by < size]
    return lax.ppermute(array, axis, pairs)


def shortened(array):

    def short(part):
        return part.astype(jnp.bfloat16) if part.dtype == jnp.float32 else part

    return jax.tree.map(short, array)


def times_rows(left, right):
    return lax.dot_general(
        left, right, (((1,), (1,)), ((), ())), preferred_element_type=jnp.float32
    )


def times_cols(left, right):
    return lax.dot_general(
        left, right, (((0,), (0,)), ((), ())), preferred_element_type=jnp.float32
    )


def finish(d_normed, x_float, scale_r, d_mixed, norm_gain):
    inner_sum = jnp.mean(d_normed * norm_gain * x_float, axis=-1, keepdims=True)
    return (
        d_mixed.astype(jnp.float32)
        + scale_r * norm_gain * d_normed
        - x_float * scale_r**3 * inner_sum
    )


def exchange_kernel(plan, heads, first_owner, *refs):
    count = len(plan)
    sources, targets = refs[:count], refs[count : 2 * count]
    send_sems, recv_sems, own_sem = refs[2 * count :]
    axes = sorted({axis for axis, _ in plan})
    barrier = pltpu.get_barrier_semaphore()
    greeted = 0
    for axis in axes:
        size = lax.axis_size(axis)
        for step in range(1, size):
            peer = lax.rem(lax.axis_index(axis) + step, size)
            pl.semaphore_signal(
                barrier, inc=1, device_id={axis: peer}, device_id_type=pl.DeviceIdType.MESH
            )
            greeted += 1
    pl.semaphore_wait(barrier, greeted)

    def owns(place):
        return (place >= first_owner) & (place < first_owner + heads)

    def when(condition, action):
        if condition is None:
            action()
        else:
            pl.when(condition)(action)

    finals = []
    for item, (axis, kind) in enumerate(plan):
        source, target = sources[item], targets[item]
        size = lax.axis_size(axis)
        me = lax.axis_index(axis)
        for step in list(range(1, size)) + [0]:
            peer = lax.rem(me + step, size)
            origin = lax.rem(me + size - step, size)
            send_if = recv_if = None
            if kind == "all":
                piece, slot = source.at[peer], target.at[me]
            elif kind == "same":
                piece, slot = source, target.at[me]
            elif kind == "to_heads":
                piece = source.at[jnp.clip(peer - first_owner, 0, heads - 1)]
                slot = target.at[me]
                send_if, recv_if = owns(peer), owns(me)
            else:
                piece = source.at[peer]
                slot = target.at[jnp.clip(me - first_owner, 0, heads - 1)]
                send_if, recv_if = owns(me), owns(origin)
            if step == 0:
                copy = pltpu.make_async_copy(piece, slot, own_sem.at[item])
                when(send_if, copy.start)
                finals.append((send_if, copy.wait))
            else:
                copy = pltpu.make_async_remote_copy(
                    src_ref=piece,
                    dst_ref=slot,
                    send_sem=send_sems.at[item, step],
                    recv_sem=recv_sems.at[item, step],
                    device_id={axis: peer},
                    device_id_type=pl.DeviceIdType.MESH,
                )
                when(send_if, copy.start)
                finals.append((send_if, copy.wait_send))
                finals.append((recv_if, copy.wait_recv))
    for condition, action in finals:
        when(condition, action)


def exchange(collective, items, heads=1):
    plan, shapes = [], []
    most = 1
    for array, axis, kind in items:
        size = lax.axis_size(axis)
        most = max(most, size)
        plan.append((axis, kind))
        tail = array.shape if kind == "same" else array.shape[1:]
        lead = heads if kind == "from_heads" else size
        shapes.append(jax.ShapeDtypeStruct((lead, *tail), array.dtype))
    first_owner = (lax.axis_size("seq") - heads) // 2
    return pl.pallas_call(
        functools.partial(exchange_kernel, tuple(plan), heads, first_owner),
        out_shape=shapes,
        in_specs=[pl.BlockSpec(memory_space=pl.ANY)] * len(plan),
        out_specs=[pl.BlockSpec(memory_space=pl.ANY)] * len(plan),
        scratch_shapes=[
            pltpu.SemaphoreType.DMA((len(plan), most)),
            pltpu.SemaphoreType.DMA((len(plan), most)),
            pltpu.SemaphoreType.DMA((len(plan),)),
        ],
        compiler_params=pltpu.CompilerParams(collective_id=collective, has_side_effects=True),
    )(*[array for array, _, _ in items])


def attention_kernel(heads, tile, kv_ref, qd_ref, low_ref, dqa_ref, dkv_ref, probs, d_kv):
    size = lax.axis_size("seq")
    first_owner = (size - heads) // 2
    me = lax.axis_index("seq")

    @pl.when((me >= first_owner) & (me < first_owner + heads))
    def _():
        tiles = kv_ref.shape[0] // tile
        d_kv[...] = jnp.zeros_like(d_kv)
        low_half = lax.broadcasted_iota(jnp.int32, (tile, LANES), 1) < HEAD
        row = lax.broadcasted_iota(jnp.int32, (tile, tile), 0)
        col = lax.broadcasted_iota(jnp.int32, (tile, tile), 1)

        def query_step(i, _):
            here = pl.ds(pl.multiple_of(i * tile, tile), tile)
            both = qd_ref[here, :]
            query = jnp.where(low_half, both, jnp.zeros_like(both))
            d_att = jnp.where(low_half, jnp.zeros_like(both), both)
            lowest = jnp.maximum(low_ref[0:1, here], i * tile + col[0:1, :] - (WIN - 1))

            def score_step(j, top):
                there = pl.ds(pl.multiple_of(j * tile, tile), tile)
                scores = times_rows(kv_ref[there, :], query)
                pos_k = j * tile + row
                allowed = (pos_k >= lowest) & (pos_k <= i * tile + col)
                scores = jnp.where(allowed, scores, -1e30)
                probs[j] = scores
                return jnp.maximum(top, jnp.max(scores, axis=0, keepdims=True))

            top = lax.fori_loop(
                0, i + 1, score_step, jnp.full((1, tile), -1e30, jnp.float32)
            )

            def raise_step(j, total):
                raised = jnp.exp(probs[j] - top)
                probs[j] = raised
                return total + jnp.sum(raised, axis=0, keepdims=True)

            total = lax.fori_loop(0, i + 1, raise_step, jnp.zeros((1, tile), jnp.float32))
            inverse = 1.0 / total

            def forward_step(j, acc):
                there = pl.ds(pl.multiple_of(j * tile, tile), tile)
                short = (probs[j] * inverse).astype(jnp.bfloat16)
                d_kv[there, :] += jnp.dot(short, d_att, preferred_element_type=jnp.float32)
                return acc + times_cols(short, kv_ref[there, :])

            zero = jnp.zeros((tile, LANES), jnp.float32)
            attended = lax.fori_loop(0, i + 1, forward_step, zero).astype(jnp.bfloat16)
            product = attended.astype(jnp.float32) * d_att.astype(jnp.float32)
            delta = jnp.sum(product.T, axis=0, keepdims=True)

            def backward_step(j, acc):
                there = pl.ds(pl.multiple_of(j * tile, tile), tile)
                d_probs = times_rows(kv_ref[there, :], d_att)
                d_scores = (probs[j] * inverse * (d_probs - delta)).astype(jnp.bfloat16)
                d_kv[there, :] += jnp.dot(d_scores, query, preferred_element_type=jnp.float32)
                return acc + times_cols(d_scores, kv_ref[there, :])

            d_query = lax.fori_loop(0, i + 1, backward_step, zero) * HEAD ** (-0.5)
            dqa_ref[here, :] = jnp.where(low_half, d_query.astype(jnp.bfloat16), attended)
            return 0

        lax.fori_loop(0, tiles, query_step, 0)
        dkv_ref[...] = d_kv[...].astype(jnp.bfloat16)


def attention(heads, kv, qd, low):
    total = kv.shape[0]
    tile = next(size for size in (256, 128) if total % size == 0)
    whole = pl.BlockSpec(memory_space=pltpu.VMEM)
    return pl.pallas_call(
        functools.partial(attention_kernel, heads, tile),
        out_shape=[jax.ShapeDtypeStruct(kv.shape, jnp.bfloat16)] * 2,
        in_specs=[whole] * 3,
        out_specs=[whole] * 2,
        scratch_shapes=[
            pltpu.VMEM((total // tile, tile, tile), jnp.float32),
            pltpu.VMEM((total, LANES), jnp.float32),
        ],
        compiler_params=pltpu.CompilerParams(vmem_limit_bytes=32 * 1024 * 1024),
    )(kv, qd, low)


def by_heads(left, right):
    rows = left.shape[0]
    pair = [part.reshape(rows, -1, HEAD) for part in (left, right)]
    return jnp.concatenate(pair, axis=2).transpose(1, 0, 2)


def from_heads(pair):
    rows = pair.shape[1]
    flat = pair.transpose(1, 0, 2)
    return flat[:, :, :HEAD].reshape(rows, -1), flat[:, :, HEAD:].reshape(rows, -1)


def by_head_owner(
    tokens, norm_gain, w_query, w_key, w_value, w_out, w_shorten, first_key, d_faces
):
    tok_rows, model_width = tokens.shape
    face_rows = tok_rows // 9
    heads = w_query.shape[1] // HEAD
    seq_count, mp_count = lax.axis_size("seq"), lax.axis_size("mp")
    chunk = w_shorten.shape[0] // mp_count
    padded = -(-chunk // 128) * 128
    tok_total = tok_rows * seq_count
    faces_total = face_rows * seq_count

    bounds = jnp.broadcast_to(jnp.pad(first_key, (0, -face_rows % 128))[None], (8, -(-face_rows // 128) * 128))
    all_d_faces, all_bounds = exchange(
        1, [(d_faces, "seq", "same"), (bounds, "seq", "same")]
    )
    low = jnp.repeat(all_bounds[:, 0, :face_rows].reshape(faces_total), 9)[None]

    shorten = jnp.pad(
        w_shorten.reshape(mp_count, chunk, -1), ((0, 0), (0, padded - chunk), (0, 0))
    )
    d_partial = jnp.einsum(
        "fc,mkc->mfk",
        all_d_faces.reshape(faces_total, -1),
        shorten,
        preferred_element_type=jnp.float32,
    ).astype(jnp.bfloat16)

    x_float = tokens.astype(jnp.float32)
    scale_r = lax.rsqrt(jnp.mean(x_float * x_float, axis=-1, keepdims=True) + 1e-05)
    normed = (x_float * scale_r * norm_gain).astype(jnp.bfloat16)
    query = jnp.dot(normed, w_query, preferred_element_type=jnp.float32).astype(jnp.bfloat16)
    key = jnp.dot(normed, w_key, preferred_element_type=jnp.float32).astype(jnp.bfloat16)
    value = jnp.dot(normed, w_value, preferred_element_type=jnp.float32).astype(jnp.bfloat16)

    d_pieces, kv = exchange(
        2, [(d_partial, "mp", "all"), (by_heads(key, value), "seq", "to_heads")], heads
    )
    d_chunk = jnp.sum(d_pieces.astype(jnp.float32), axis=0).astype(jnp.bfloat16)
    (d_chunk,) = exchange(
        3, [(d_chunk.reshape(seq_count, face_rows, padded), "seq", "all")]
    )
    (d_whole,) = exchange(4, [(d_chunk, "mp", "same")])
    d_mixed = (
        d_whole[..., :chunk].transpose(2, 1, 0, 3).reshape(tok_rows, model_width)
    )
    d_attended = times_rows(d_mixed, w_out).astype(jnp.bfloat16)
    (qd,) = exchange(
        5,
        [(by_heads(query * jnp.bfloat16(HEAD ** (-0.5)), d_attended), "seq", "to_heads")],
        heads,
    )
    dqa, dkv = attention(
        heads, kv.reshape(tok_total, LANES), qd.reshape(tok_total, LANES), low
    )
    block = (seq_count, tok_rows, LANES)
    dqa, dkv = exchange(
        6,
        [(dqa.reshape(block), "seq", "from_heads"), (dkv.reshape(block), "seq", "from_heads")],
        heads,
    )
    d_query, attended = from_heads(dqa)
    d_key, d_value = from_heads(dkv)
    projected = jnp.dot(attended, w_out, preferred_element_type=jnp.float32).astype(jnp.bfloat16)
    projected = projected.reshape(mp_count, tok_rows // mp_count, model_width)
    part_normed = times_rows(d_query, w_query)
    part_normed = part_normed + times_rows(d_key, w_key)
    part_normed = part_normed + times_rows(d_value, w_value)
    part_normed = part_normed.astype(jnp.bfloat16).reshape(projected.shape)
    projected, part_normed = exchange(
        7, [(projected, "mp", "all"), (part_normed, "mp", "all")]
    )
    projected = jnp.sum(projected.astype(jnp.float32), axis=0).astype(jnp.bfloat16)
    part_normed = jnp.sum(part_normed.astype(jnp.float32), axis=0).astype(jnp.bfloat16)
    summed, d_normed = exchange(
        8, [(projected, "mp", "same"), (part_normed, "mp", "same")]
    )
    d_normed = d_normed.reshape(tok_rows, model_width).astype(jnp.float32)
    summed = summed.reshape(tok_rows, model_width).astype(jnp.float32)
    mixed = (x_float + summed).astype(jnp.bfloat16)
    mixed = mixed.reshape(face_rows, seq_count, -1).transpose(1, 0, 2)
    (mixed,) = exchange(9, [(mixed, "seq", "all")])
    partial = jnp.dot(
        mixed.reshape(faces_total, -1), w_shorten, preferred_element_type=jnp.float32
    )
    partial = partial.astype(jnp.bfloat16).reshape(seq_count, face_rows, -1)
    (partial,) = exchange(10, [(partial, "seq", "all")])
    faces = jnp.sum(partial.astype(jnp.float32), axis=0).astype(jnp.bfloat16)
    d_tokens = finish(d_normed, x_float, scale_r, d_mixed, norm_gain).astype(jnp.bfloat16)
    return (faces, d_tokens)


def by_window(tokens, norm_gain, w_query, w_key, w_value, w_out, w_shorten, first_key, d_faces):
    tok_rows = tokens.shape[0]
    model_width = tokens.shape[1]
    face_rows = tok_rows // 9
    local_width = w_query.shape[1]
    local_heads = local_width // HEAD
    seq_count = lax.axis_size("seq")
    hops = min(-(-WIN // tok_rows), seq_count - 1)
    levels = hops.bit_length()
    seq_index = lax.axis_index("seq")
    x_float = tokens.astype(jnp.float32)
    scale_r = lax.rsqrt(jnp.mean(x_float * x_float, axis=-1, keepdims=True) + 1e-05)
    normed = (x_float * scale_r * norm_gain).astype(jnp.bfloat16)
    query = jnp.dot(normed, w_query, preferred_element_type=jnp.float32).astype(jnp.bfloat16)
    key = jnp.dot(normed, w_key, preferred_element_type=jnp.float32).astype(jnp.bfloat16)
    value = jnp.dot(normed, w_value, preferred_element_type=jnp.float32).astype(jnp.bfloat16)
    stacked_key = key[None]
    stacked_value = value[None]
    for level in range(levels):
        reach_by = 1 << level
        came_key, came_value = shifted((stacked_key, stacked_value), "seq", reach_by)
        stacked_key = jnp.concatenate([stacked_key, came_key], axis=0)
        stacked_value = jnp.concatenate([stacked_value, came_value], axis=0)
    anchors = seq_index - jnp.arange(hops + 1, dtype=jnp.int32)
    block_count = stacked_key.shape[0]
    key_total = block_count * tok_rows
    pos_q = seq_index * tok_rows + jnp.arange(tok_rows, dtype=jnp.int32)
    pos_k = (anchors[:, None] * tok_rows + jnp.arange(tok_rows, dtype=jnp.int32)[None, :]).reshape(
        key_total
    )
    lower_bound = jnp.repeat(first_key, 9)
    allowed = (
        (pos_k[None, :] >= lower_bound[:, None])
        & (pos_k[None, :] <= pos_q[:, None])
        & (pos_q[:, None] - pos_k[None, :] < WIN)
    )
    query_heads = query.reshape(tok_rows, local_heads, HEAD).transpose(1, 0, 2)
    key_heads = stacked_key.reshape(key_total, local_heads, HEAD).transpose(1, 0, 2)
    value_heads = stacked_value.reshape(key_total, local_heads, HEAD).transpose(1, 0, 2)

    def head_probs(query_head, key_head):
        scores = times_rows(query_head, key_head) * HEAD ** (-0.5)
        scores = jnp.where(allowed, scores, -1e30)
        row_top = jnp.max(scores, axis=-1, keepdims=True)
        raised = jnp.exp(scores - row_top)
        return raised / jnp.sum(raised, axis=-1, keepdims=True)

    def head_forward(operands):
        query_head, key_head, value_head = operands
        probs = head_probs(query_head, key_head)
        return jnp.dot(
            probs.astype(jnp.bfloat16), value_head, preferred_element_type=jnp.float32
        ).astype(jnp.bfloat16)

    att_heads = lax.map(head_forward, (query_heads, key_heads, value_heads))
    attended = att_heads.transpose(1, 0, 2).reshape(tok_rows, local_width)
    projected = jnp.dot(attended, w_out, preferred_element_type=jnp.float32)
    summed = lax.psum(projected.astype(jnp.bfloat16), "mp").astype(jnp.float32)
    mixed = (x_float + summed).astype(jnp.bfloat16)
    mixed_faces = mixed.reshape(face_rows, 9 * model_width)
    full_shorten = lax.all_gather(w_shorten, "seq", axis=0, tiled=True)
    face_sum = jnp.dot(mixed_faces, full_shorten, preferred_element_type=jnp.float32)
    d_partial = times_rows(d_faces, full_shorten)
    faces = face_sum.astype(jnp.bfloat16)
    d_mixed = lax.psum(d_partial, "mp").astype(jnp.bfloat16).reshape(tok_rows, model_width)
    d_attended = times_rows(d_mixed, w_out).astype(jnp.bfloat16)
    d_att_heads = d_attended.reshape(tok_rows, local_heads, HEAD).transpose(1, 0, 2)

    def head_backward(operands):
        query_head, key_head, value_head, d_att_head, att_head = operands
        probs = head_probs(query_head, key_head)
        d_probs = times_rows(d_att_head, value_head)
        row_delta = jnp.sum(d_att_head.astype(jnp.float32) * att_head.astype(jnp.float32), axis=-1)
        d_scores = (probs * (d_probs - row_delta[:, None])).astype(jnp.bfloat16)
        d_query_head = (
            jnp.dot(d_scores, key_head, preferred_element_type=jnp.float32) * HEAD ** (-0.5)
        ).astype(jnp.bfloat16)
        d_key_head = times_cols(d_scores, query_head) * HEAD ** (-0.5)
        d_value_head = times_cols(probs.astype(jnp.bfloat16), d_att_head)
        return (d_query_head, d_key_head, d_value_head)

    d_query_heads, d_key_heads, d_value_heads = lax.map(
        head_backward, (query_heads, key_heads, value_heads, d_att_heads, att_heads)
    )
    d_query = d_query_heads.transpose(1, 0, 2).reshape(tok_rows, local_width)
    d_key_parts = d_key_heads.transpose(1, 0, 2).reshape(block_count, tok_rows, local_width)
    d_value_parts = d_value_heads.transpose(1, 0, 2).reshape(block_count, tok_rows, local_width)
    spare_blocks = (1 << levels) - block_count
    filler = jnp.zeros((spare_blocks, tok_rows, local_width), jnp.float32)
    parts_key = jnp.concatenate([d_key_parts, filler], axis=0)
    parts_value = jnp.concatenate([d_value_parts, filler], axis=0)
    for level in reversed(range(levels)):
        reach_by = 1 << level
        came_key, came_value = shifted(
            (
                shortened(parts_key[reach_by : 2 * reach_by]),
                shortened(parts_value[reach_by : 2 * reach_by]),
            ),
            "seq",
            -reach_by,
        )
        parts_key = parts_key[:reach_by] + came_key
        parts_value = parts_value[:reach_by] + came_value
    acc_key, acc_value = (parts_key[0], parts_value[0])
    d_key = acc_key.astype(jnp.bfloat16)
    d_value = acc_value.astype(jnp.bfloat16)
    part_normed = times_rows(d_query, w_query)
    part_normed = part_normed + times_rows(d_key, w_key)
    part_normed = part_normed + times_rows(d_value, w_value)
    d_normed = lax.psum(part_normed.astype(jnp.bfloat16), "mp").astype(jnp.float32)
    d_tokens = finish(d_normed, x_float, scale_r, d_mixed, norm_gain).astype(jnp.bfloat16)
    return (faces, d_tokens)


def local(*arrays):
    heads = arrays[2].shape[1] // HEAD
    seq_count = lax.axis_size("seq")
    if heads <= seq_count < 2 * heads:
        return by_head_owner(*arrays)
    return by_window(*arrays)


def solution(mesh):
    in_specs = (
        P("seq", None),
        P(),
        P(None, "mp"),
        P(None, "mp"),
        P(None, "mp"),
        P("mp", None),
        P("seq", "mp"),
        P("seq"),
        P("seq", "mp"),
    )
    out_specs = (P("seq", "mp"), P("seq", None))
    return jax.shard_map(local, mesh=mesh, in_specs=in_specs, out_specs=out_specs, check_vma=False)
```

```python
import functools

import jax
import jax.numpy as jnp
from jax import lax
from jax.experimental import pallas as pl
from jax.experimental.pallas import tpu as pltpu
from jax.sharding import PartitionSpec as P

HEAD = 64
WIN = 4096
LANES = 2 * HEAD


def shifted(array, axis, by):
    size = lax.axis_size(axis)
    pairs = [(i, i + by) for i in range(size) if 0 <= i + by < size]
    return lax.ppermute(array, axis, pairs)


def shortened(array):

    def short(part):
        return part.astype(jnp.bfloat16) if part.dtype == jnp.float32 else part

    return jax.tree.map(short, array)


def times_rows(left, right):
    return lax.dot_general(
        left, right, (((1,), (1,)), ((), ())), preferred_element_type=jnp.float32
    )


def times_cols(left, right):
    return lax.dot_general(
        left, right, (((0,), (0,)), ((), ())), preferred_element_type=jnp.float32
    )


def finish(d_normed, x_float, scale_r, d_mixed, norm_gain):
    inner_sum = jnp.mean(d_normed * norm_gain * x_float, axis=-1, keepdims=True)
    return (
        d_mixed.astype(jnp.float32)
        + scale_r * norm_gain * d_normed
        - x_float * scale_r**3 * inner_sum
    )


def exchange_kernel(plan, heads, first_owner, *refs):
    count = len(plan)
    sources, targets = refs[:count], refs[count : 2 * count]
    send_sems, recv_sems, own_sem = refs[2 * count : 2 * count + 3]
    spares = refs[2 * count + 3 :]
    barrier = pltpu.get_barrier_semaphore()
    greeted = 0
    for axis in sorted({axis for axis, _ in plan}):
        size = lax.axis_size(axis)
        for step in range(1, size):
            peer = lax.rem(lax.axis_index(axis) + step, size)
            pl.semaphore_signal(
                barrier, inc=1, device_id={axis: peer}, device_id_type=pl.DeviceIdType.MESH
            )
            greeted += 1
    pl.semaphore_wait(barrier, greeted)

    def owns(place):
        return (place >= first_owner) & (place < first_owner + heads)

    def when(condition, action):
        if condition is None:
            action()
        else:
            pl.when(condition)(action)

    def remote(item, step, piece, slot, axis, peer):
        return pltpu.make_async_remote_copy(
            src_ref=piece,
            dst_ref=slot,
            send_sem=send_sems.at[item, step],
            recv_sem=recv_sems.at[item, step],
            device_id={axis: peer},
            device_id_type=pl.DeviceIdType.MESH,
        )

    finals = []
    paired = []
    for item, (axis, kind) in sorted(enumerate(plan), key=lambda pair: pair[1][1] not in PAIRED):
        source, target = sources[item], targets[item]
        size = lax.axis_size(axis)
        me = lax.axis_index(axis)
        if kind in PAIRED:
            near = me + 1 - 2 * lax.rem(me, 2)
            far = lax.rem(me + 2, 4)
            far_near = lax.rem(near + 2, 4)
            link = functools.partial(remote, item)
            if kind == "gather":
                own = pltpu.make_async_copy(source, target.at[me], own_sem.at[item])
                own.start()
                first = [
                    link(0, source, target.at[me], axis, far),
                    link(1, source, target.at[me], axis, near),
                ]
                second = link(2, target.at[far], target.at[far], axis, near)
            else:
                came, joined, crossed = spares[:3]
                spares = spares[3:]
                first = [
                    link(0, source.at[far_near], came.at[0], axis, near),
                    link(1, source.at[near], came.at[1], axis, near),
                ]
                second = link(2, joined, crossed, axis, far)
                own = None
            for copy in first:
                copy.start()
            paired.append((item, kind, me, far, first, second, own))
            if kind == "reduce":
                paired[-1] += (came, joined, crossed)
            continue
        for step in list(range(1, size)) + [0]:
            peer = lax.rem(me + step, size)
            origin = lax.rem(me + size - step, size)
            send_if = recv_if = None
            if kind == "all":
                piece, slot = source.at[peer], target.at[me]
            elif kind == "same":
                piece, slot = source, target.at[me]
            elif kind == "to_heads":
                piece = source.at[jnp.clip(peer - first_owner, 0, heads - 1)]
                slot = target.at[me]
                send_if, recv_if = owns(peer), owns(me)
            else:
                piece = source.at[peer]
                slot = target.at[jnp.clip(me - first_owner, 0, heads - 1)]
                send_if, recv_if = owns(me), owns(origin)
            if step == 0:
                copy = pltpu.make_async_copy(piece, slot, own_sem.at[item])
                when(send_if, copy.start)
                finals.append((send_if, copy.wait))
            else:
                copy = remote(item, step, piece, slot, axis, peer)
                when(send_if, copy.start)
                finals.append((send_if, copy.wait_send))
                finals.append((recv_if, copy.wait_recv))

    def added(left, right):
        return (left.astype(jnp.float32) + right.astype(jnp.float32)).astype(jnp.bfloat16)

    for item, kind, me, far, first, second, own, *held in paired:
        if kind == "gather":
            first[0].wait_recv()
            second.start()
        else:
            came, joined, crossed = held
            first[0].wait_recv()
            joined[...] = added(sources[item][far], came[0])
            second.start()
    for item, kind, me, far, first, second, own, *held in paired:
        if kind == "gather":
            first[0].wait_send()
            first[1].wait()
            second.wait()
            own.wait()
        else:
            came, joined, crossed = held
            first[1].wait_recv()
            mine = sources[item][me].astype(jnp.float32) + came[1].astype(jnp.float32)
            second.wait_recv()
            targets[item][...] = (mine + crossed[...].astype(jnp.float32)).astype(jnp.bfloat16)
            first[0].wait_send()
            first[1].wait_send()
            second.wait_send()
    for condition, action in finals:
        when(condition, action)


PAIRED = ("gather", "reduce")


def exchange(collective, items, heads=1):
    plan, shapes, spares, in_specs, out_specs = [], [], [], [], []
    most = 3
    for array, axis, kind in items:
        size = lax.axis_size(axis)
        most = max(most, size)
        plan.append((axis, kind))
        tail = array.shape if kind in ("same", "gather") else array.shape[1:]
        lead = heads if kind == "from_heads" else size
        space = pl.ANY
        if kind == "reduce":
            shapes.append(jax.ShapeDtypeStruct(tail, array.dtype))
            spares.append(pltpu.VMEM((2, *tail), array.dtype))
            spares += [pltpu.VMEM(tail, array.dtype)] * 2
            space = pltpu.VMEM
        else:
            shapes.append(jax.ShapeDtypeStruct((lead, *tail), array.dtype))
        in_specs.append(pl.BlockSpec(memory_space=space))
        out_specs.append(pl.BlockSpec(memory_space=space))
    first_owner = (lax.axis_size("seq") - heads) // 2
    return pl.pallas_call(
        functools.partial(exchange_kernel, tuple(plan), heads, first_owner),
        out_shape=shapes,
        in_specs=in_specs,
        out_specs=out_specs,
        scratch_shapes=[
            pltpu.SemaphoreType.DMA((len(plan), most)),
            pltpu.SemaphoreType.DMA((len(plan), most)),
            pltpu.SemaphoreType.DMA((len(plan),)),
            *spares,
        ],
        compiler_params=pltpu.CompilerParams(
            collective_id=collective, has_side_effects=True, vmem_limit_bytes=24 * 1024 * 1024
        ),
    )(*[array for array, _, _ in items])


def when_owner(heads, action):
    first_owner = (lax.axis_size("seq") - heads) // 2
    me = lax.axis_index("seq")
    pl.when((me >= first_owner) & (me < first_owner + heads))(action)


def rolled(array):
    return pltpu.roll(array.astype(jnp.float32), HEAD, 1)


def unpack(packed_ref, flat_ref, upper):
    blocks, half, _ = packed_ref.shape
    low_half = lax.broadcasted_iota(jnp.int32, (half, LANES), 1) < HEAD
    for block in range(blocks):
        packed = packed_ref[block]
        other = rolled(packed).astype(packed.dtype)
        parts = (other, packed) if upper else (packed, other)
        zero = jnp.zeros_like(packed)
        for place, part in enumerate(parts):
            part = jnp.where(low_half, zero, part) if upper else jnp.where(low_half, part, zero)
            flat_ref[pl.ds((2 * block + place) * half, half), :] = part


def pack(flat_ref, packed_ref, upper):
    blocks, half, _ = packed_ref.shape
    low_half = lax.broadcasted_iota(jnp.int32, (half, LANES), 1) < HEAD
    for block in range(blocks):
        top = flat_ref[pl.ds(2 * block * half, half), :]
        bottom = flat_ref[pl.ds((2 * block + 1) * half, half), :]
        if upper:
            top = rolled(top).astype(top.dtype)
        else:
            bottom = rolled(bottom).astype(top.dtype)
        packed_ref[block] = jnp.where(low_half, top, bottom)


def masked_scores(kv, query, lowest, key_start, query_start):
    scores = times_rows(kv, query)
    pos_k = key_start + lax.broadcasted_iota(jnp.int32, scores.shape, 0)
    pos_q = query_start + lax.broadcasted_iota(jnp.int32, (1, scores.shape[1]), 1)
    allowed = (pos_k >= jnp.maximum(lowest, pos_q - (WIN - 1))) & (pos_k <= pos_q)
    return jnp.where(allowed, scores, -1e30)


def forward_kernel(
    heads, tile, span, kv_ref, packed_ref, low_ref, out_ref, query_ref, att_ref, top_ref, inv_ref
):
    def run():
        unpack(packed_ref, query_ref, False)
        high_half = lax.broadcasted_iota(jnp.int32, (tile, LANES), 1) >= HEAD

        def query_step(i, _):
            here = pl.ds(pl.multiple_of(i * tile, tile), tile)
            query = query_ref[here, :]
            lowest = low_ref[0:1, here]

            def key_step(j, carry):
                top, total, acc = carry
                kv = kv_ref[pl.ds(pl.multiple_of(j * span, span), span), :]
                scores = masked_scores(kv, query, lowest, j * span, i * tile)
                new_top = jnp.maximum(top, jnp.max(scores, axis=0, keepdims=True))
                raised = jnp.exp(scores - new_top)
                shrink = jnp.exp(top - new_top)
                total = total * shrink + jnp.sum(raised, axis=0, keepdims=True)
                acc = acc * shrink + times_cols(kv, raised.astype(jnp.bfloat16))
                return new_top, total, acc

            start = (
                jnp.full((1, tile), -1e30, jnp.float32),
                jnp.zeros((1, tile), jnp.float32),
                jnp.zeros((LANES, tile), jnp.float32),
            )
            top, total, acc = lax.fori_loop(0, (i * tile + tile - 1) // span + 1, key_step, start)
            inverse = 1.0 / total
            top_ref[0:1, here] = top
            inv_ref[0:1, here] = inverse
            attended = (acc * inverse).T.astype(jnp.bfloat16)
            att_ref[here, :] = jnp.where(high_half, attended, jnp.zeros_like(attended))
            return 0

        lax.fori_loop(0, kv_ref.shape[0] // tile, query_step, 0)
        pack(att_ref, out_ref, True)

    when_owner(heads, run)


def backward_kernel(
    heads, tile, span, kv_ref, query_ref, packed_ref, low_ref, att_ref, top_ref, inv_ref,
    dq_out, dkv_out, d_att_ref, dq_ref, d_kv,
):
    def run():
        unpack(packed_ref, d_att_ref, True)
        d_kv[...] = jnp.zeros_like(d_kv)

        def query_step(i, _):
            here = pl.ds(pl.multiple_of(i * tile, tile), tile)
            query, d_att = query_ref[here, :], d_att_ref[here, :]
            lowest, top, inverse = low_ref[0:1, here], top_ref[0:1, here], inv_ref[0:1, here]
            product = att_ref[here, :].astype(jnp.float32) * d_att.astype(jnp.float32)
            delta = jnp.sum(product.T, axis=0, keepdims=True)

            def key_step(j, acc):
                there = pl.ds(pl.multiple_of(j * span, span), span)
                kv = kv_ref[there, :]
                scores = masked_scores(kv, query, lowest, j * span, i * tile)
                probs = jnp.exp(scores - top) * inverse
                d_probs = times_rows(kv, d_att)
                d_scores = (probs * (d_probs - delta)).astype(jnp.bfloat16)
                d_kv[there, :] += jnp.dot(
                    d_scores, query, preferred_element_type=jnp.float32
                ) + jnp.dot(
                    probs.astype(jnp.bfloat16), d_att, preferred_element_type=jnp.float32
                )
                return acc + times_cols(kv, d_scores)

            zero = jnp.zeros((LANES, tile), jnp.float32)
            acc = lax.fori_loop(0, (i * tile + tile - 1) // span + 1, key_step, zero)
            dq_ref[here, :] = (acc * HEAD ** (-0.5)).T.astype(jnp.bfloat16)
            return 0

        lax.fori_loop(0, kv_ref.shape[0] // tile, query_step, 0)
        dkv_out[...] = d_kv[...].astype(jnp.bfloat16)
        pack(dq_ref, dq_out, False)

    when_owner(heads, run)


def tiling(total):
    tile = next(size for size in (256, 128) if total % size == 0)
    return tile, tile * (3 if total % (3 * tile) == 0 else 1)


def plain_call(body, arrays, shapes, scratch=()):
    whole = pl.BlockSpec(memory_space=pltpu.VMEM)
    return pl.pallas_call(
        body,
        out_shape=[jax.ShapeDtypeStruct(*shape) for shape in shapes],
        in_specs=[whole] * len(arrays),
        out_specs=[whole] * len(shapes),
        scratch_shapes=list(scratch),
        compiler_params=pltpu.CompilerParams(vmem_limit_bytes=32 * 1024 * 1024),
    )(*arrays)


def by_heads(left, right):
    rows = left.shape[0]
    pair = [part.reshape(rows, -1, HEAD) for part in (left, right)]
    return jnp.concatenate(pair, axis=2).transpose(1, 0, 2)


def packed_heads(array):
    half = array.shape[0] // 2
    return by_heads(array[:half], array[half:])


def from_heads(pair):
    rows = pair.shape[1]
    flat = pair.transpose(1, 0, 2)
    return flat[:, :, :HEAD].reshape(rows, -1), flat[:, :, HEAD:].reshape(rows, -1)


def unpacked_heads(pair):
    return jnp.concatenate(from_heads(pair), axis=0)


def by_head_owner(
    tokens, norm_gain, w_query, w_key, w_value, w_out, w_shorten, first_key, d_faces
):
    tok_rows, model_width = tokens.shape
    face_rows = tok_rows // 9
    heads = w_query.shape[1] // HEAD
    seq_count, mp_count = lax.axis_size("seq"), lax.axis_size("mp")
    chunk = w_shorten.shape[0] // mp_count
    padded = -(-chunk // 128) * 128
    tok_total = tok_rows * seq_count
    faces_total = face_rows * seq_count
    bf16, f32 = jnp.bfloat16, jnp.float32

    wide = -(-face_rows // 128) * 128
    bounds = jnp.broadcast_to(jnp.pad(first_key, (0, wide - face_rows))[None], (8, wide))
    all_d_faces, all_bounds = exchange(
        1, [(d_faces, "seq", "same"), (bounds, "seq", "same")]
    )
    low = jnp.repeat(all_bounds[:, 0, :face_rows].reshape(faces_total), 9)[None]

    shorten = jnp.pad(
        w_shorten.reshape(mp_count, chunk, -1), ((0, 0), (0, padded - chunk), (0, 0))
    )
    d_partial = jnp.einsum(
        "fc,mkc->mfk",
        all_d_faces.reshape(faces_total, -1),
        shorten,
        preferred_element_type=f32,
    ).astype(bf16)

    x_float = tokens.astype(f32)
    scale_r = lax.rsqrt(jnp.mean(x_float * x_float, axis=-1, keepdims=True) + 1e-05)
    normed = (x_float * scale_r * norm_gain).astype(bf16)
    query = jnp.dot(normed, w_query, preferred_element_type=f32).astype(bf16)
    key = jnp.dot(normed, w_key, preferred_element_type=f32).astype(bf16)
    value = jnp.dot(normed, w_value, preferred_element_type=f32).astype(bf16)

    kv, packed_query, d_chunk = exchange(
        2,
        [
            (by_heads(key, value), "seq", "to_heads"),
            (packed_heads(query * bf16(HEAD ** (-0.5))), "seq", "to_heads"),
            (d_partial, "mp", "reduce"),
        ],
        heads,
    )
    kv = kv.reshape(tok_total, LANES)
    tile, span = tiling(tok_total)
    flat = ((tok_total, LANES), bf16)
    folded = ((seq_count, tok_rows // 2, LANES), bf16)
    line = ((1, tok_total), f32)
    att_packed, query_flat, att_flat, top, inverse = plain_call(
        functools.partial(forward_kernel, heads, tile, span),
        (kv, packed_query, low),
        (folded, flat, flat, line, line),
    )
    att_packed, d_chunk = exchange(
        3,
        [
            (att_packed, "seq", "from_heads"),
            (d_chunk.reshape(seq_count, face_rows, padded), "seq", "all"),
        ],
        heads,
    )
    attended = unpacked_heads(att_packed)
    projected = jnp.dot(attended, w_out, preferred_element_type=f32) + x_float / mp_count
    projected = projected.astype(bf16).reshape(face_rows, seq_count, mp_count, chunk)
    projected = jnp.pad(projected, ((0, 0), (0, 0), (0, 0), (0, padded - chunk)))
    projected = projected.transpose(2, 1, 0, 3).reshape(mp_count, faces_total, padded)
    d_whole, mixed = exchange(4, [(d_chunk, "mp", "gather"), (projected, "mp", "reduce")])
    d_mixed = d_whole[..., :chunk].transpose(2, 1, 0, 3).reshape(tok_rows, model_width)
    d_attended = times_rows(d_mixed, w_out).astype(bf16)
    d_att_packed, mixed = exchange(
        5,
        [
            (packed_heads(d_attended), "seq", "to_heads"),
            (mixed.reshape(seq_count, face_rows, padded), "seq", "all"),
        ],
        heads,
    )
    d_query, d_kv = plain_call(
        functools.partial(backward_kernel, heads, tile, span),
        (kv, query_flat, d_att_packed, low, att_flat, top, inverse),
        (folded, flat),
        [pltpu.VMEM(*flat), pltpu.VMEM(*flat), pltpu.VMEM(flat[0], f32)],
    )
    d_query, d_kv, mixed = exchange(
        6,
        [
            (d_query, "seq", "from_heads"),
            (d_kv.reshape(seq_count, tok_rows, LANES), "seq", "from_heads"),
            (mixed, "mp", "gather"),
        ],
        heads,
    )
    partial = jnp.einsum(
        "mfk,mkc->fc",
        mixed.reshape(mp_count, faces_total, padded),
        shorten,
        preferred_element_type=f32,
    )
    partial = partial.astype(bf16).reshape(seq_count, face_rows, -1)
    d_query = unpacked_heads(d_query)
    d_key, d_value = from_heads(d_kv)
    part_normed = times_rows(d_query, w_query)
    part_normed = part_normed + times_rows(d_key, w_key)
    part_normed = part_normed + times_rows(d_value, w_value)
    part_normed = part_normed.astype(bf16).reshape(mp_count, tok_rows // mp_count, model_width)
    part_normed, partial = exchange(
        7, [(part_normed, "mp", "reduce"), (partial, "seq", "all")]
    )
    (d_normed,) = exchange(8, [(part_normed, "mp", "gather")])
    faces = jnp.sum(partial.astype(f32), axis=0).astype(bf16)
    d_normed = d_normed.reshape(tok_rows, model_width).astype(f32)
    d_tokens = finish(d_normed, x_float, scale_r, d_mixed, norm_gain).astype(bf16)
    return (faces, d_tokens)


def by_window(tokens, norm_gain, w_query, w_key, w_value, w_out, w_shorten, first_key, d_faces):
    tok_rows = tokens.shape[0]
    model_width = tokens.shape[1]
    face_rows = tok_rows // 9
    local_width = w_query.shape[1]
    local_heads = local_width // HEAD
    seq_count = lax.axis_size("seq")
    hops = min(-(-WIN // tok_rows), seq_count - 1)
    levels = hops.bit_length()
    seq_index = lax.axis_index("seq")
    x_float = tokens.astype(jnp.float32)
    scale_r = lax.rsqrt(jnp.mean(x_float * x_float, axis=-1, keepdims=True) + 1e-05)
    normed = (x_float * scale_r * norm_gain).astype(jnp.bfloat16)
    query = jnp.dot(normed, w_query, preferred_element_type=jnp.float32).astype(jnp.bfloat16)
    key = jnp.dot(normed, w_key, preferred_element_type=jnp.float32).astype(jnp.bfloat16)
    value = jnp.dot(normed, w_value, preferred_element_type=jnp.float32).astype(jnp.bfloat16)
    stacked_key = key[None]
    stacked_value = value[None]
    for level in range(levels):
        reach_by = 1 << level
        came_key, came_value = shifted((stacked_key, stacked_value), "seq", reach_by)
        stacked_key = jnp.concatenate([stacked_key, came_key], axis=0)
        stacked_value = jnp.concatenate([stacked_value, came_value], axis=0)
    anchors = seq_index - jnp.arange(hops + 1, dtype=jnp.int32)
    block_count = stacked_key.shape[0]
    key_total = block_count * tok_rows
    pos_q = seq_index * tok_rows + jnp.arange(tok_rows, dtype=jnp.int32)
    pos_k = (anchors[:, None] * tok_rows + jnp.arange(tok_rows, dtype=jnp.int32)[None, :]).reshape(
        key_total
    )
    lower_bound = jnp.repeat(first_key, 9)
    allowed = (
        (pos_k[None, :] >= lower_bound[:, None])
        & (pos_k[None, :] <= pos_q[:, None])
        & (pos_q[:, None] - pos_k[None, :] < WIN)
    )
    query_heads = query.reshape(tok_rows, local_heads, HEAD).transpose(1, 0, 2)
    key_heads = stacked_key.reshape(key_total, local_heads, HEAD).transpose(1, 0, 2)
    value_heads = stacked_value.reshape(key_total, local_heads, HEAD).transpose(1, 0, 2)

    def head_probs(query_head, key_head):
        scores = times_rows(query_head, key_head) * HEAD ** (-0.5)
        scores = jnp.where(allowed, scores, -1e30)
        row_top = jnp.max(scores, axis=-1, keepdims=True)
        raised = jnp.exp(scores - row_top)
        return raised / jnp.sum(raised, axis=-1, keepdims=True)

    def head_forward(operands):
        query_head, key_head, value_head = operands
        probs = head_probs(query_head, key_head)
        return jnp.dot(
            probs.astype(jnp.bfloat16), value_head, preferred_element_type=jnp.float32
        ).astype(jnp.bfloat16)

    att_heads = lax.map(head_forward, (query_heads, key_heads, value_heads))
    attended = att_heads.transpose(1, 0, 2).reshape(tok_rows, local_width)
    projected = jnp.dot(attended, w_out, preferred_element_type=jnp.float32)
    summed = lax.psum(projected.astype(jnp.bfloat16), "mp").astype(jnp.float32)
    mixed = (x_float + summed).astype(jnp.bfloat16)
    mixed_faces = mixed.reshape(face_rows, 9 * model_width)
    full_shorten = lax.all_gather(w_shorten, "seq", axis=0, tiled=True)
    face_sum = jnp.dot(mixed_faces, full_shorten, preferred_element_type=jnp.float32)
    d_partial = times_rows(d_faces, full_shorten)
    faces = face_sum.astype(jnp.bfloat16)
    d_mixed = lax.psum(d_partial, "mp").astype(jnp.bfloat16).reshape(tok_rows, model_width)
    d_attended = times_rows(d_mixed, w_out).astype(jnp.bfloat16)
    d_att_heads = d_attended.reshape(tok_rows, local_heads, HEAD).transpose(1, 0, 2)

    def head_backward(operands):
        query_head, key_head, value_head, d_att_head, att_head = operands
        probs = head_probs(query_head, key_head)
        d_probs = times_rows(d_att_head, value_head)
        row_delta = jnp.sum(d_att_head.astype(jnp.float32) * att_head.astype(jnp.float32), axis=-1)
        d_scores = (probs * (d_probs - row_delta[:, None])).astype(jnp.bfloat16)
        d_query_head = (
            jnp.dot(d_scores, key_head, preferred_element_type=jnp.float32) * HEAD ** (-0.5)
        ).astype(jnp.bfloat16)
        d_key_head = times_cols(d_scores, query_head) * HEAD ** (-0.5)
        d_value_head = times_cols(probs.astype(jnp.bfloat16), d_att_head)
        return (d_query_head, d_key_head, d_value_head)

    d_query_heads, d_key_heads, d_value_heads = lax.map(
        head_backward, (query_heads, key_heads, value_heads, d_att_heads, att_heads)
    )
    d_query = d_query_heads.transpose(1, 0, 2).reshape(tok_rows, local_width)
    d_key_parts = d_key_heads.transpose(1, 0, 2).reshape(block_count, tok_rows, local_width)
    d_value_parts = d_value_heads.transpose(1, 0, 2).reshape(block_count, tok_rows, local_width)
    spare_blocks = (1 << levels) - block_count
    filler = jnp.zeros((spare_blocks, tok_rows, local_width), jnp.float32)
    parts_key = jnp.concatenate([d_key_parts, filler], axis=0)
    parts_value = jnp.concatenate([d_value_parts, filler], axis=0)
    for level in reversed(range(levels)):
        reach_by = 1 << level
        came_key, came_value = shifted(
            (
                shortened(parts_key[reach_by : 2 * reach_by]),
                shortened(parts_value[reach_by : 2 * reach_by]),
            ),
            "seq",
            -reach_by,
        )
        parts_key = parts_key[:reach_by] + came_key
        parts_value = parts_value[:reach_by] + came_value
    acc_key, acc_value = (parts_key[0], parts_value[0])
    d_key = acc_key.astype(jnp.bfloat16)
    d_value = acc_value.astype(jnp.bfloat16)
    part_normed = times_rows(d_query, w_query)
    part_normed = part_normed + times_rows(d_key, w_key)
    part_normed = part_normed + times_rows(d_value, w_value)
    d_normed = lax.psum(part_normed.astype(jnp.bfloat16), "mp").astype(jnp.float32)
    d_tokens = finish(d_normed, x_float, scale_r, d_mixed, norm_gain).astype(jnp.bfloat16)
    return (faces, d_tokens)


def local(*arrays):
    heads = arrays[2].shape[1] // HEAD
    seq_count = lax.axis_size("seq")
    if heads <= seq_count < 2 * heads and lax.axis_size("mp") == 4:
        return by_head_owner(*arrays)
    return by_window(*arrays)


def solution(mesh):
    in_specs = (
        P("seq", None),
        P(),
        P(None, "mp"),
        P(None, "mp"),
        P(None, "mp"),
        P("mp", None),
        P("seq", "mp"),
        P("seq"),
        P("seq", "mp"),
    )
    out_specs = (P("seq", "mp"), P("seq", None))
    return jax.shard_map(local, mesh=mesh, in_specs=in_specs, out_specs=out_specs, check_vma=False)
```

```python
import functools

import jax
import jax.numpy as jnp
from jax import lax
from jax.experimental import pallas as pl
from jax.experimental.pallas import tpu as pltpu
from jax.sharding import PartitionSpec as P

HEAD = 64
WIN = 4096
LANES = 2 * HEAD


def shifted(array, axis, by):
    size = lax.axis_size(axis)
    pairs = [(i, i + by) for i in range(size) if 0 <= i + by < size]
    return lax.ppermute(array, axis, pairs)


def shortened(array):

    def short(part):
        return part.astype(jnp.bfloat16) if part.dtype == jnp.float32 else part

    return jax.tree.map(short, array)


def times_rows(left, right):
    return lax.dot_general(
        left, right, (((1,), (1,)), ((), ())), preferred_element_type=jnp.float32
    )


def times_cols(left, right):
    return lax.dot_general(
        left, right, (((0,), (0,)), ((), ())), preferred_element_type=jnp.float32
    )


def finish(d_normed, x_float, scale_r, d_mixed, norm_gain):
    inner_sum = jnp.mean(d_normed * norm_gain * x_float, axis=-1, keepdims=True)
    return (
        d_mixed.astype(jnp.float32)
        + scale_r * norm_gain * d_normed
        - x_float * scale_r**3 * inner_sum
    )


def exchange_kernel(plan, heads, first_owner, *refs):
    count = len(plan)
    sources, targets = refs[:count], refs[count : 2 * count]
    send_sems, recv_sems, own_sem = refs[2 * count : 2 * count + 3]
    spares = refs[2 * count + 3 :]
    barrier = pltpu.get_barrier_semaphore()
    greeted = 0
    for axis in sorted({axis for axis, _ in plan}):
        size = lax.axis_size(axis)
        for step in range(1, size):
            peer = lax.rem(lax.axis_index(axis) + step, size)
            pl.semaphore_signal(
                barrier, inc=1, device_id={axis: peer}, device_id_type=pl.DeviceIdType.MESH
            )
            greeted += 1
    pl.semaphore_wait(barrier, greeted)

    def owns(place):
        return (place >= first_owner) & (place < first_owner + heads)

    def when(condition, action):
        if condition is None:
            action()
        else:
            pl.when(condition)(action)

    def remote(item, step, piece, slot, axis, peer):
        return pltpu.make_async_remote_copy(
            src_ref=piece,
            dst_ref=slot,
            send_sem=send_sems.at[item, step],
            recv_sem=recv_sems.at[item, step],
            device_id={axis: peer},
            device_id_type=pl.DeviceIdType.MESH,
        )

    finals = []
    paired = []
    for item, (axis, kind) in sorted(enumerate(plan), key=lambda pair: pair[1][1] not in PAIRED):
        source, target = sources[item], targets[item]
        size = lax.axis_size(axis)
        me = lax.axis_index(axis)
        if kind in PAIRED:
            near = me + 1 - 2 * lax.rem(me, 2)
            far = lax.rem(me + 2, 4)
            far_near = lax.rem(near + 2, 4)
            link = functools.partial(remote, item)
            if kind == "gather":
                own = pltpu.make_async_copy(source, target.at[me], own_sem.at[item])
                own.start()
                first = [
                    link(0, source, target.at[me], axis, far),
                    link(1, source, target.at[me], axis, near),
                ]
                second = link(2, target.at[far], target.at[far], axis, near)
            else:
                came, joined, crossed = spares[:3]
                spares = spares[3:]
                first = [
                    link(0, source.at[far_near], came.at[0], axis, near),
                    link(1, source.at[near], came.at[1], axis, near),
                ]
                second = link(2, joined, crossed, axis, far)
                own = None
            for copy in first:
                copy.start()
            paired.append((item, kind, me, far, first, second, own))
            if kind == "reduce":
                paired[-1] += (came, joined, crossed)
            continue
        for step in list(range(1, size)) + [0]:
            peer = lax.rem(me + step, size)
            origin = lax.rem(me + size - step, size)
            send_if = recv_if = None
            if kind == "all":
                piece, slot = source.at[peer], target.at[me]
            elif kind == "same":
                piece, slot = source, target.at[me]
            elif kind == "to_heads":
                piece = source.at[jnp.clip(peer - first_owner, 0, heads - 1)]
                slot = target.at[me]
                send_if, recv_if = owns(peer), owns(me)
            else:
                piece = source.at[peer]
                slot = target.at[jnp.clip(me - first_owner, 0, heads - 1)]
                send_if, recv_if = owns(me), owns(origin)
            if step == 0:
                copy = pltpu.make_async_copy(piece, slot, own_sem.at[item])
                when(send_if, copy.start)
                finals.append((send_if, copy.wait))
            else:
                copy = remote(item, step, piece, slot, axis, peer)
                when(send_if, copy.start)
                finals.append((send_if, copy.wait_send))
                finals.append((recv_if, copy.wait_recv))

    def added(left, right):
        return (left.astype(jnp.float32) + right.astype(jnp.float32)).astype(jnp.bfloat16)

    for item, kind, me, far, first, second, own, *held in paired:
        if kind == "gather":
            first[0].wait_recv()
            second.start()
        else:
            came, joined, crossed = held
            first[0].wait_recv()
            joined[...] = added(sources[item][far], came[0])
            second.start()
    for item, kind, me, far, first, second, own, *held in paired:
        if kind == "gather":
            first[0].wait_send()
            first[1].wait()
            second.wait()
            own.wait()
        else:
            came, joined, crossed = held
            first[1].wait_recv()
            mine = sources[item][me].astype(jnp.float32) + came[1].astype(jnp.float32)
            second.wait_recv()
            targets[item][...] = (mine + crossed[...].astype(jnp.float32)).astype(jnp.bfloat16)
            first[0].wait_send()
            first[1].wait_send()
            second.wait_send()
    for condition, action in finals:
        when(condition, action)


PAIRED = ("gather", "reduce")


def exchange(collective, items, heads=1):
    plan, shapes, spares, in_specs, out_specs = [], [], [], [], []
    most = 3
    for array, axis, kind in items:
        size = lax.axis_size(axis)
        most = max(most, size)
        plan.append((axis, kind))
        tail = array.shape if kind in ("same", "gather") else array.shape[1:]
        lead = heads if kind == "from_heads" else size
        space = pl.ANY
        if kind == "reduce":
            shapes.append(jax.ShapeDtypeStruct(tail, array.dtype))
            spares.append(pltpu.VMEM((2, *tail), array.dtype))
            spares += [pltpu.VMEM(tail, array.dtype)] * 2
            space = pltpu.VMEM
        else:
            shapes.append(jax.ShapeDtypeStruct((lead, *tail), array.dtype))
        in_specs.append(pl.BlockSpec(memory_space=space))
        out_specs.append(pl.BlockSpec(memory_space=space))
    first_owner = (lax.axis_size("seq") - heads) // 2
    return pl.pallas_call(
        functools.partial(exchange_kernel, tuple(plan), heads, first_owner),
        out_shape=shapes,
        in_specs=in_specs,
        out_specs=out_specs,
        scratch_shapes=[
            pltpu.SemaphoreType.DMA((len(plan), most)),
            pltpu.SemaphoreType.DMA((len(plan), most)),
            pltpu.SemaphoreType.DMA((len(plan),)),
            *spares,
        ],
        compiler_params=pltpu.CompilerParams(
            collective_id=collective, has_side_effects=True, vmem_limit_bytes=24 * 1024 * 1024
        ),
    )(*[array for array, _, _ in items])


def when_owner(heads, action):
    first_owner = (lax.axis_size("seq") - heads) // 2
    me = lax.axis_index("seq")
    pl.when((me >= first_owner) & (me < first_owner + heads))(action)


def rolled(array):
    return pltpu.roll(array.astype(jnp.float32), HEAD, 1)


def unpack(packed_ref, flat_ref, upper):
    blocks, half, _ = packed_ref.shape
    low_half = lax.broadcasted_iota(jnp.int32, (half, LANES), 1) < HEAD
    for block in range(blocks):
        packed = packed_ref[block]
        other = rolled(packed).astype(packed.dtype)
        parts = (other, packed) if upper else (packed, other)
        zero = jnp.zeros_like(packed)
        for place, part in enumerate(parts):
            part = jnp.where(low_half, zero, part) if upper else jnp.where(low_half, part, zero)
            flat_ref[pl.ds((2 * block + place) * half, half), :] = part


def pack(flat_ref, packed_ref, upper):
    blocks, half, _ = packed_ref.shape
    low_half = lax.broadcasted_iota(jnp.int32, (half, LANES), 1) < HEAD
    for block in range(blocks):
        top = flat_ref[pl.ds(2 * block * half, half), :]
        bottom = flat_ref[pl.ds((2 * block + 1) * half, half), :]
        if upper:
            top = rolled(top).astype(top.dtype)
        else:
            bottom = rolled(bottom).astype(top.dtype)
        packed_ref[block] = jnp.where(low_half, top, bottom)


def masked_scores(kv, query, lowest, key_start, query_start):
    scores = times_rows(kv, query)
    pos_k = key_start + lax.broadcasted_iota(jnp.int32, scores.shape, 0)
    pos_q = query_start + lax.broadcasted_iota(jnp.int32, (1, scores.shape[1]), 1)
    allowed = (pos_k >= jnp.maximum(lowest, pos_q - (WIN - 1))) & (pos_k <= pos_q)
    return jnp.where(allowed, scores, -1e30)


def forward_kernel(
    heads, tile, span, kv_ref, packed_ref, low_ref, out_ref, query_ref, att_ref, top_ref, inv_ref
):
    def run():
        unpack(packed_ref, query_ref, False)
        high_half = lax.broadcasted_iota(jnp.int32, (tile, LANES), 1) >= HEAD

        def query_step(i, _):
            here = pl.ds(pl.multiple_of(i * tile, tile), tile)
            query = query_ref[here, :]
            lowest = low_ref[0:1, here]

            def key_step(j, carry):
                top, total, acc = carry
                kv = kv_ref[pl.ds(pl.multiple_of(j * span, span), span), :]
                scores = masked_scores(kv, query, lowest, j * span, i * tile)
                new_top = jnp.maximum(top, jnp.max(scores, axis=0, keepdims=True))
                raised = jnp.exp(scores - new_top)
                shrink = jnp.exp(top - new_top)
                total = total * shrink + jnp.sum(raised, axis=0, keepdims=True)
                acc = acc * shrink + times_cols(kv, raised.astype(jnp.bfloat16))
                return new_top, total, acc

            start = (
                jnp.full((1, tile), -1e30, jnp.float32),
                jnp.zeros((1, tile), jnp.float32),
                jnp.zeros((LANES, tile), jnp.float32),
            )
            top, total, acc = lax.fori_loop(0, (i * tile + tile - 1) // span + 1, key_step, start)
            inverse = 1.0 / total
            top_ref[0:1, here] = top
            inv_ref[0:1, here] = inverse
            attended = (acc * inverse).T.astype(jnp.bfloat16)
            att_ref[here, :] = jnp.where(high_half, attended, jnp.zeros_like(attended))
            return 0

        lax.fori_loop(0, kv_ref.shape[0] // tile, query_step, 0)
        pack(att_ref, out_ref, True)

    when_owner(heads, run)


def backward_kernel(
    heads, tile, span, kv_ref, query_ref, packed_ref, low_ref, att_ref, top_ref, inv_ref,
    dq_out, dkv_out, d_att_ref, dq_ref, d_kv,
):
    def run():
        unpack(packed_ref, d_att_ref, True)
        d_kv[...] = jnp.zeros_like(d_kv)

        def query_step(i, _):
            here = pl.ds(pl.multiple_of(i * tile, tile), tile)
            query, d_att = query_ref[here, :], d_att_ref[here, :]
            lowest, top, inverse = low_ref[0:1, here], top_ref[0:1, here], inv_ref[0:1, here]
            product = att_ref[here, :].astype(jnp.float32) * d_att.astype(jnp.float32)
            delta = jnp.sum(product.T, axis=0, keepdims=True)

            def key_step(j, acc):
                there = pl.ds(pl.multiple_of(j * span, span), span)
                kv = kv_ref[there, :]
                scores = masked_scores(kv, query, lowest, j * span, i * tile)
                probs = jnp.exp(scores - top) * inverse
                d_probs = times_rows(kv, d_att)
                d_scores = (probs * (d_probs - delta)).astype(jnp.bfloat16)
                d_kv[there, :] += jnp.dot(
                    d_scores, query, preferred_element_type=jnp.float32
                ) + jnp.dot(
                    probs.astype(jnp.bfloat16), d_att, preferred_element_type=jnp.float32
                )
                return acc + times_cols(kv, d_scores)

            zero = jnp.zeros((LANES, tile), jnp.float32)
            acc = lax.fori_loop(0, (i * tile + tile - 1) // span + 1, key_step, zero)
            dq_ref[here, :] = (acc * HEAD ** (-0.5)).T.astype(jnp.bfloat16)
            return 0

        lax.fori_loop(0, kv_ref.shape[0] // tile, query_step, 0)
        dkv_out[...] = d_kv[...].astype(jnp.bfloat16)
        pack(dq_ref, dq_out, False)

    when_owner(heads, run)


def tiling(total):
    tile = next(size for size in (256, 128) if total % size == 0)
    return tile, tile * (3 if total % (3 * tile) == 0 else 1)


def plain_call(body, arrays, shapes, scratch=()):
    whole = pl.BlockSpec(memory_space=pltpu.VMEM)
    return pl.pallas_call(
        body,
        out_shape=[jax.ShapeDtypeStruct(*shape) for shape in shapes],
        in_specs=[whole] * len(arrays),
        out_specs=[whole] * len(shapes),
        scratch_shapes=list(scratch),
        compiler_params=pltpu.CompilerParams(vmem_limit_bytes=32 * 1024 * 1024),
    )(*arrays)


def twist(left, right):
    low_half = lax.broadcasted_iota(jnp.int32, left.shape, 1) < HEAD
    first = jnp.where(low_half, left, rolled(right).astype(left.dtype))
    second = jnp.where(low_half, rolled(left).astype(left.dtype), right)
    return first, second


def split_pairs(left, right, out_ref):
    for pair in range(left.shape[1] // LANES):
        lanes = slice(pair * LANES, (pair + 1) * LANES)
        out_ref[2 * pair], out_ref[2 * pair + 1] = twist(left[:, lanes], right[:, lanes])


def join_pairs(ref):
    lefts, rights = zip(*(twist(ref[head], ref[head + 1]) for head in range(0, ref.shape[0], 2)))
    return jnp.concatenate(lefts, axis=1), jnp.concatenate(rights, axis=1)


def rounded_dot(left, right):
    return jnp.dot(left, right, preferred_element_type=jnp.float32).astype(jnp.bfloat16)


def prepare_kernel(x_ref, gain_ref, wq_ref, wk_ref, wv_ref, kv_ref, packed_ref):
    x = x_ref[...].astype(jnp.float32)
    scale_r = lax.rsqrt(jnp.mean(x * x, axis=-1, keepdims=True) + 1e-05)
    normed = (x * scale_r * gain_ref[...]).astype(jnp.bfloat16)
    split_pairs(rounded_dot(normed, wk_ref[...]), rounded_dot(normed, wv_ref[...]), kv_ref)
    query = rounded_dot(normed, wq_ref[...]) * jnp.bfloat16(HEAD ** (-0.5))
    half = query.shape[0] // 2
    split_pairs(query[:half], query[half:], packed_ref)


def project_kernel(parts, packed_ref, w_ref, x_ref, out_ref):
    top, bottom = join_pairs(packed_ref)
    half = top.shape[0]
    for rows, part in ((slice(0, half), top), (slice(half, 2 * half), bottom)):
        product = jnp.dot(part, w_ref[...], preferred_element_type=jnp.float32)
        x = x_ref[rows, :].astype(jnp.float32) * (1.0 / parts)
        out_ref[rows, :] = (product + x).astype(jnp.bfloat16)


def d_attended_kernel(d_mixed_ref, w_ref, packed_ref):
    d_attended = times_rows(d_mixed_ref[...], w_ref[...]).astype(jnp.bfloat16)
    half = d_attended.shape[0] // 2
    split_pairs(d_attended[:half], d_attended[half:], packed_ref)


def d_normed_kernel(dq_ref, dkv_ref, wq_ref, wk_ref, wv_ref, out_ref):
    d_query = jnp.concatenate(join_pairs(dq_ref), axis=0)
    d_key, d_value = join_pairs(dkv_ref)
    total = times_rows(d_query, wq_ref[...]) + times_rows(d_key, wk_ref[...])
    out_ref[...] = (total + times_rows(d_value, wv_ref[...])).astype(jnp.bfloat16)


def by_head_owner(
    tokens, norm_gain, w_query, w_key, w_value, w_out, w_shorten, first_key, d_faces
):
    tok_rows, model_width = tokens.shape
    face_rows = tok_rows // 9
    width = w_query.shape[1]
    heads = width // HEAD
    seq_count, mp_count = lax.axis_size("seq"), lax.axis_size("mp")
    share = face_rows // mp_count
    halves = 16 // share
    chunk = w_shorten.shape[0] // halves
    padded = -(-chunk // 128) * 128
    tok_total = tok_rows * seq_count
    faces_total = face_rows * seq_count
    bf16, f32 = jnp.bfloat16, jnp.float32

    wide = -(-face_rows // 128) * 128
    bounds = jnp.broadcast_to(jnp.pad(first_key, (0, wide - face_rows))[None], (8, wide))
    all_d_faces, all_bounds = exchange(
        1, [(d_faces, "seq", "same"), (bounds, "seq", "same")]
    )
    low = jnp.repeat(all_bounds[:, 0, :face_rows].reshape(faces_total), 9)[None]

    shorten = jnp.pad(
        w_shorten.reshape(halves, chunk, -1), ((0, 0), (0, padded - chunk), (0, 0))
    )
    by_share = all_d_faces.reshape(seq_count, mp_count, share, -1).transpose(1, 0, 2, 3)
    by_share = by_share.reshape(faces_total, -1)
    d_partial = [
        times_rows(by_share, shorten[half])
        .astype(bf16)
        .reshape(mp_count, seq_count, share, padded)
        for half in range(halves)
    ]
    d_partial = jnp.concatenate(d_partial, axis=2)
    d_partial = d_partial.reshape(mp_count, seq_count * halves * share, padded)

    half_rows = tok_rows // 2
    kv, packed_query = plain_call(
        prepare_kernel,
        (tokens, norm_gain[None], w_query, w_key, w_value),
        (((heads, tok_rows, LANES), bf16), ((heads, half_rows, LANES), bf16)),
    )
    kv, packed_query, d_chunk = exchange(
        2,
        [
            (kv, "seq", "to_heads"),
            (packed_query, "seq", "to_heads"),
            (d_partial, "mp", "reduce"),
        ],
        heads,
    )
    kv = kv.reshape(tok_total, LANES)
    tile, span = tiling(tok_total)
    flat = ((tok_total, LANES), bf16)
    folded = ((seq_count, half_rows, LANES), bf16)
    line = ((1, tok_total), f32)
    att_packed, query_flat, att_flat, top, inverse = plain_call(
        functools.partial(forward_kernel, heads, tile, span),
        (kv, packed_query, low),
        (folded, flat, flat, line, line),
    )
    moved = (seq_count, halves * share, padded)
    att_packed, d_chunk = exchange(
        3,
        [(att_packed, "seq", "from_heads"), (d_chunk.reshape(moved), "seq", "all")],
        heads,
    )
    (projected,) = plain_call(
        functools.partial(project_kernel, mp_count),
        (att_packed, w_out, tokens),
        [((tok_rows, model_width), bf16)],
    )
    d_chunk = d_chunk.reshape(seq_count, halves, share, padded)[..., :chunk]
    d_chunk = d_chunk.transpose(2, 0, 1, 3).reshape(tok_rows // mp_count, model_width)
    d_mixed, mixed = exchange(
        4,
        [
            (d_chunk, "mp", "gather"),
            (projected.reshape(mp_count, *d_chunk.shape), "mp", "reduce"),
        ],
    )
    d_mixed = d_mixed.reshape(tok_rows, model_width)
    (d_att_packed,) = plain_call(
        d_attended_kernel, (d_mixed, w_out), [((heads, half_rows, LANES), bf16)]
    )
    mixed = mixed.reshape(share, seq_count, halves, chunk).transpose(1, 2, 0, 3)
    mixed = jnp.pad(mixed, ((0, 0), (0, 0), (0, 0), (0, padded - chunk))).reshape(moved)
    d_att_packed, mixed = exchange(
        5, [(d_att_packed, "seq", "to_heads"), (mixed, "seq", "all")], heads
    )
    d_query, d_kv = plain_call(
        functools.partial(backward_kernel, heads, tile, span),
        (kv, query_flat, d_att_packed, low, att_flat, top, inverse),
        (folded, flat),
        [pltpu.VMEM(*flat), pltpu.VMEM(*flat), pltpu.VMEM(flat[0], f32)],
    )
    d_query, d_kv, mixed = exchange(
        6,
        [
            (d_query, "seq", "from_heads"),
            (d_kv.reshape(seq_count, tok_rows, LANES), "seq", "from_heads"),
            (mixed, "mp", "gather"),
        ],
        heads,
    )
    (part_normed,) = plain_call(
        d_normed_kernel,
        (d_query, d_kv, w_query, w_key, w_value),
        [((tok_rows, model_width), bf16)],
    )
    mixed = mixed.reshape(mp_count, seq_count, halves, share, padded)
    partial = sum(
        jnp.dot(
            mixed[:, :, half].reshape(faces_total, padded),
            shorten[half],
            preferred_element_type=f32,
        )
        for half in range(halves)
    )
    partial = partial.astype(bf16).reshape(mp_count, seq_count, share, -1)
    partial = partial.transpose(1, 0, 2, 3).reshape(seq_count, face_rows, -1)
    part_normed, partial = exchange(
        7,
        [
            (part_normed.reshape(mp_count, *d_chunk.shape), "mp", "reduce"),
            (partial, "seq", "all"),
        ],
    )
    (d_normed,) = exchange(8, [(part_normed, "mp", "gather")])
    faces = jnp.sum(partial.astype(f32), axis=0).astype(bf16)
    d_normed = d_normed.reshape(tok_rows, model_width).astype(f32)
    x_float = tokens.astype(f32)
    scale_r = lax.rsqrt(jnp.mean(x_float * x_float, axis=-1, keepdims=True) + 1e-05)
    d_tokens = finish(d_normed, x_float, scale_r, d_mixed, norm_gain).astype(bf16)
    return (faces, d_tokens)


def by_window(tokens, norm_gain, w_query, w_key, w_value, w_out, w_shorten, first_key, d_faces):
    tok_rows = tokens.shape[0]
    model_width = tokens.shape[1]
    face_rows = tok_rows // 9
    local_width = w_query.shape[1]
    local_heads = local_width // HEAD
    seq_count = lax.axis_size("seq")
    hops = min(-(-WIN // tok_rows), seq_count - 1)
    levels = hops.bit_length()
    seq_index = lax.axis_index("seq")
    x_float = tokens.astype(jnp.float32)
    scale_r = lax.rsqrt(jnp.mean(x_float * x_float, axis=-1, keepdims=True) + 1e-05)
    normed = (x_float * scale_r * norm_gain).astype(jnp.bfloat16)
    query = jnp.dot(normed, w_query, preferred_element_type=jnp.float32).astype(jnp.bfloat16)
    key = jnp.dot(normed, w_key, preferred_element_type=jnp.float32).astype(jnp.bfloat16)
    value = jnp.dot(normed, w_value, preferred_element_type=jnp.float32).astype(jnp.bfloat16)
    stacked_key = key[None]
    stacked_value = value[None]
    for level in range(levels):
        reach_by = 1 << level
        came_key, came_value = shifted((stacked_key, stacked_value), "seq", reach_by)
        stacked_key = jnp.concatenate([stacked_key, came_key], axis=0)
        stacked_value = jnp.concatenate([stacked_value, came_value], axis=0)
    anchors = seq_index - jnp.arange(hops + 1, dtype=jnp.int32)
    block_count = stacked_key.shape[0]
    key_total = block_count * tok_rows
    pos_q = seq_index * tok_rows + jnp.arange(tok_rows, dtype=jnp.int32)
    pos_k = (anchors[:, None] * tok_rows + jnp.arange(tok_rows, dtype=jnp.int32)[None, :]).reshape(
        key_total
    )
    lower_bound = jnp.repeat(first_key, 9)
    allowed = (
        (pos_k[None, :] >= lower_bound[:, None])
        & (pos_k[None, :] <= pos_q[:, None])
        & (pos_q[:, None] - pos_k[None, :] < WIN)
    )
    query_heads = query.reshape(tok_rows, local_heads, HEAD).transpose(1, 0, 2)
    key_heads = stacked_key.reshape(key_total, local_heads, HEAD).transpose(1, 0, 2)
    value_heads = stacked_value.reshape(key_total, local_heads, HEAD).transpose(1, 0, 2)

    def head_probs(query_head, key_head):
        scores = times_rows(query_head, key_head) * HEAD ** (-0.5)
        scores = jnp.where(allowed, scores, -1e30)
        row_top = jnp.max(scores, axis=-1, keepdims=True)
        raised = jnp.exp(scores - row_top)
        return raised / jnp.sum(raised, axis=-1, keepdims=True)

    def head_forward(operands):
        query_head, key_head, value_head = operands
        probs = head_probs(query_head, key_head)
        return jnp.dot(
            probs.astype(jnp.bfloat16), value_head, preferred_element_type=jnp.float32
        ).astype(jnp.bfloat16)

    att_heads = lax.map(head_forward, (query_heads, key_heads, value_heads))
    attended = att_heads.transpose(1, 0, 2).reshape(tok_rows, local_width)
    projected = jnp.dot(attended, w_out, preferred_element_type=jnp.float32)
    summed = lax.psum(projected.astype(jnp.bfloat16), "mp").astype(jnp.float32)
    mixed = (x_float + summed).astype(jnp.bfloat16)
    mixed_faces = mixed.reshape(face_rows, 9 * model_width)
    full_shorten = lax.all_gather(w_shorten, "seq", axis=0, tiled=True)
    face_sum = jnp.dot(mixed_faces, full_shorten, preferred_element_type=jnp.float32)
    d_partial = times_rows(d_faces, full_shorten)
    faces = face_sum.astype(jnp.bfloat16)
    d_mixed = lax.psum(d_partial, "mp").astype(jnp.bfloat16).reshape(tok_rows, model_width)
    d_attended = times_rows(d_mixed, w_out).astype(jnp.bfloat16)
    d_att_heads = d_attended.reshape(tok_rows, local_heads, HEAD).transpose(1, 0, 2)

    def head_backward(operands):
        query_head, key_head, value_head, d_att_head, att_head = operands
        probs = head_probs(query_head, key_head)
        d_probs = times_rows(d_att_head, value_head)
        row_delta = jnp.sum(d_att_head.astype(jnp.float32) * att_head.astype(jnp.float32), axis=-1)
        d_scores = (probs * (d_probs - row_delta[:, None])).astype(jnp.bfloat16)
        d_query_head = (
            jnp.dot(d_scores, key_head, preferred_element_type=jnp.float32) * HEAD ** (-0.5)
        ).astype(jnp.bfloat16)
        d_key_head = times_cols(d_scores, query_head) * HEAD ** (-0.5)
        d_value_head = times_cols(probs.astype(jnp.bfloat16), d_att_head)
        return (d_query_head, d_key_head, d_value_head)

    d_query_heads, d_key_heads, d_value_heads = lax.map(
        head_backward, (query_heads, key_heads, value_heads, d_att_heads, att_heads)
    )
    d_query = d_query_heads.transpose(1, 0, 2).reshape(tok_rows, local_width)
    d_key_parts = d_key_heads.transpose(1, 0, 2).reshape(block_count, tok_rows, local_width)
    d_value_parts = d_value_heads.transpose(1, 0, 2).reshape(block_count, tok_rows, local_width)
    spare_blocks = (1 << levels) - block_count
    filler = jnp.zeros((spare_blocks, tok_rows, local_width), jnp.float32)
    parts_key = jnp.concatenate([d_key_parts, filler], axis=0)
    parts_value = jnp.concatenate([d_value_parts, filler], axis=0)
    for level in reversed(range(levels)):
        reach_by = 1 << level
        came_key, came_value = shifted(
            (
                shortened(parts_key[reach_by : 2 * reach_by]),
                shortened(parts_value[reach_by : 2 * reach_by]),
            ),
            "seq",
            -reach_by,
        )
        parts_key = parts_key[:reach_by] + came_key
        parts_value = parts_value[:reach_by] + came_value
    acc_key, acc_value = (parts_key[0], parts_value[0])
    d_key = acc_key.astype(jnp.bfloat16)
    d_value = acc_value.astype(jnp.bfloat16)
    part_normed = times_rows(d_query, w_query)
    part_normed = part_normed + times_rows(d_key, w_key)
    part_normed = part_normed + times_rows(d_value, w_value)
    d_normed = lax.psum(part_normed.astype(jnp.bfloat16), "mp").astype(jnp.float32)
    d_tokens = finish(d_normed, x_float, scale_r, d_mixed, norm_gain).astype(jnp.bfloat16)
    return (faces, d_tokens)


def local(*arrays):
    heads = arrays[2].shape[1] // HEAD
    seq_count = lax.axis_size("seq")
    whole_pairs = heads % 2 == 0 and lax.axis_size("mp") == 4
    if heads <= seq_count < 2 * heads and whole_pairs:
        return by_head_owner(*arrays)
    return by_window(*arrays)


def solution(mesh):
    in_specs = (
        P("seq", None),
        P(),
        P(None, "mp"),
        P(None, "mp"),
        P(None, "mp"),
        P("mp", None),
        P("seq", "mp"),
        P("seq"),
        P("seq", "mp"),
    )
    out_specs = (P("seq", "mp"), P("seq", None))
    return jax.shard_map(local, mesh=mesh, in_specs=in_specs, out_specs=out_specs, check_vma=False)
```

```python
import functools

import jax
import jax.numpy as jnp
from jax import lax
from jax.experimental import pallas as pl
from jax.experimental.pallas import tpu as pltpu
from jax.sharding import PartitionSpec as P

HEAD = 64
WIN = 4096
LANES = 2 * HEAD


def shifted(array, axis, by):
    size = lax.axis_size(axis)
    pairs = [(i, i + by) for i in range(size) if 0 <= i + by < size]
    return lax.ppermute(array, axis, pairs)


def shortened(array):

    def short(part):
        return part.astype(jnp.bfloat16) if part.dtype == jnp.float32 else part

    return jax.tree.map(short, array)


def times_rows(left, right):
    return lax.dot_general(
        left, right, (((1,), (1,)), ((), ())), preferred_element_type=jnp.float32
    )


def times_cols(left, right):
    return lax.dot_general(
        left, right, (((0,), (0,)), ((), ())), preferred_element_type=jnp.float32
    )


def finish(d_normed, x_float, scale_r, d_mixed, norm_gain):
    inner_sum = jnp.mean(d_normed * norm_gain * x_float, axis=-1, keepdims=True)
    return (
        d_mixed.astype(jnp.float32)
        + scale_r * norm_gain * d_normed
        - x_float * scale_r**3 * inner_sum
    )


def exchange_kernel(plan, heads, first_owner, *refs):
    count = len(plan)
    sources, targets = refs[:count], refs[count : 2 * count]
    send_sems, recv_sems, own_sem = refs[2 * count : 2 * count + 3]
    spares = refs[2 * count + 3 :]
    barrier = pltpu.get_barrier_semaphore()
    greeted = 0
    for axis in sorted({axis for axis, _ in plan}):
        size = lax.axis_size(axis)
        for step in range(1, size):
            peer = lax.rem(lax.axis_index(axis) + step, size)
            pl.semaphore_signal(
                barrier, inc=1, device_id={axis: peer}, device_id_type=pl.DeviceIdType.MESH
            )
            greeted += 1
    pl.semaphore_wait(barrier, greeted)

    def owns(place):
        return (place >= first_owner) & (place < first_owner + heads)

    def when(condition, action):
        if condition is None:
            action()
        else:
            pl.when(condition)(action)

    def remote(item, step, piece, slot, axis, peer):
        return pltpu.make_async_remote_copy(
            src_ref=piece,
            dst_ref=slot,
            send_sem=send_sems.at[item, step],
            recv_sem=recv_sems.at[item, step],
            device_id={axis: peer},
            device_id_type=pl.DeviceIdType.MESH,
        )

    finals = []
    paired = []
    for item, (axis, kind) in sorted(enumerate(plan), key=lambda pair: pair[1][1] not in PAIRED):
        source, target = sources[item], targets[item]
        size = lax.axis_size(axis)
        me = lax.axis_index(axis)
        if kind in PAIRED:
            near = me + 1 - 2 * lax.rem(me, 2)
            far = lax.rem(me + 2, 4)
            far_near = lax.rem(near + 2, 4)
            link = functools.partial(remote, item)
            if kind == "gather":
                own = pltpu.make_async_copy(source, target.at[me], own_sem.at[item])
                own.start()
                first = [
                    link(0, source, target.at[me], axis, far),
                    link(1, source, target.at[me], axis, near),
                ]
                second = link(2, target.at[far], target.at[far], axis, near)
            else:
                came, joined, crossed = spares[:3]
                spares = spares[3:]
                first = [
                    link(0, source.at[far_near], came.at[0], axis, near),
                    link(1, source.at[near], came.at[1], axis, near),
                ]
                second = link(2, joined, crossed, axis, far)
                own = None
            for copy in first:
                copy.start()
            paired.append((item, kind, me, far, first, second, own))
            if kind == "reduce":
                paired[-1] += (came, joined, crossed)
            continue
        for step in list(range(1, size)) + [0]:
            peer = lax.rem(me + step, size)
            origin = lax.rem(me + size - step, size)
            send_if = recv_if = None
            if kind == "all":
                piece, slot = source.at[peer], target.at[me]
            elif kind == "same":
                piece, slot = source, target.at[me]
            elif kind == "to_heads":
                piece = source.at[jnp.clip(peer - first_owner, 0, heads - 1)]
                slot = target.at[me]
                send_if, recv_if = owns(peer), owns(me)
            else:
                piece = source.at[peer]
                slot = target.at[jnp.clip(me - first_owner, 0, heads - 1)]
                send_if, recv_if = owns(me), owns(origin)
            if step == 0:
                copy = pltpu.make_async_copy(piece, slot, own_sem.at[item])
                when(send_if, copy.start)
                finals.append((send_if, copy.wait))
            else:
                copy = remote(item, step, piece, slot, axis, peer)
                when(send_if, copy.start)
                finals.append((send_if, copy.wait_send))
                finals.append((recv_if, copy.wait_recv))

    def added(left, right):
        return (left.astype(jnp.float32) + right.astype(jnp.float32)).astype(jnp.bfloat16)

    for item, kind, me, far, first, second, own, *held in paired:
        if kind == "gather":
            first[0].wait_recv()
            second.start()
        else:
            came, joined, crossed = held
            first[0].wait_recv()
            joined[...] = added(sources[item][far], came[0])
            second.start()
    for item, kind, me, far, first, second, own, *held in paired:
        if kind == "gather":
            first[0].wait_send()
            first[1].wait()
            second.wait()
            own.wait()
        else:
            came, joined, crossed = held
            first[1].wait_recv()
            mine = sources[item][me].astype(jnp.float32) + came[1].astype(jnp.float32)
            second.wait_recv()
            targets[item][...] = (mine + crossed[...].astype(jnp.float32)).astype(jnp.bfloat16)
            first[0].wait_send()
            first[1].wait_send()
            second.wait_send()
    for condition, action in finals:
        when(condition, action)


PAIRED = ("gather", "reduce")


def exchange(collective, items, heads=1):
    plan, shapes, spares, in_specs, out_specs = [], [], [], [], []
    most = 3
    for array, axis, kind in items:
        size = lax.axis_size(axis)
        most = max(most, size)
        plan.append((axis, kind))
        tail = array.shape if kind in ("same", "gather") else array.shape[1:]
        lead = heads if kind == "from_heads" else size
        space = pl.ANY
        if kind == "reduce":
            shapes.append(jax.ShapeDtypeStruct(tail, array.dtype))
            spares.append(pltpu.VMEM((2, *tail), array.dtype))
            spares += [pltpu.VMEM(tail, array.dtype)] * 2
            space = pltpu.VMEM
        else:
            shapes.append(jax.ShapeDtypeStruct((lead, *tail), array.dtype))
        in_specs.append(pl.BlockSpec(memory_space=space))
        out_specs.append(pl.BlockSpec(memory_space=space))
    first_owner = (lax.axis_size("seq") - heads) // 2
    return pl.pallas_call(
        functools.partial(exchange_kernel, tuple(plan), heads, first_owner),
        out_shape=shapes,
        in_specs=in_specs,
        out_specs=out_specs,
        scratch_shapes=[
            pltpu.SemaphoreType.DMA((len(plan), most)),
            pltpu.SemaphoreType.DMA((len(plan), most)),
            pltpu.SemaphoreType.DMA((len(plan),)),
            *spares,
        ],
        compiler_params=pltpu.CompilerParams(
            collective_id=collective, has_side_effects=True, vmem_limit_bytes=24 * 1024 * 1024
        ),
    )(*[array for array, _, _ in items])


def when_owner(heads, action):
    first_owner = (lax.axis_size("seq") - heads) // 2
    me = lax.axis_index("seq")
    pl.when((me >= first_owner) & (me < first_owner + heads))(action)


def rolled(array):
    return pltpu.roll(array.astype(jnp.float32), HEAD, 1)


def unpack(packed_ref, flat_ref, upper):
    blocks, half, _ = packed_ref.shape
    low_half = lax.broadcasted_iota(jnp.int32, (half, LANES), 1) < HEAD
    for block in range(blocks):
        packed = packed_ref[block]
        other = rolled(packed).astype(packed.dtype)
        parts = (other, packed) if upper else (packed, other)
        zero = jnp.zeros_like(packed)
        for place, part in enumerate(parts):
            part = jnp.where(low_half, zero, part) if upper else jnp.where(low_half, part, zero)
            flat_ref[pl.ds((2 * block + place) * half, half), :] = part


def pack(flat_ref, packed_ref, upper, chosen=None):
    blocks, half, _ = packed_ref.shape
    low_half = lax.broadcasted_iota(jnp.int32, (half, LANES), 1) < HEAD
    for block in range(blocks) if chosen is None else chosen:
        top = flat_ref[pl.ds(2 * block * half, half), :]
        bottom = flat_ref[pl.ds((2 * block + 1) * half, half), :]
        if upper:
            top = rolled(top).astype(top.dtype)
        else:
            bottom = rolled(bottom).astype(top.dtype)
        packed_ref[block] = jnp.where(low_half, top, bottom)


def masked_scores(kv, query, lowest, key_start, query_start):
    scores = times_rows(kv, query)
    pos_k = key_start + lax.broadcasted_iota(jnp.int32, scores.shape, 0)
    pos_q = query_start + lax.broadcasted_iota(jnp.int32, (1, scores.shape[1]), 1)
    allowed = (pos_k >= jnp.maximum(lowest, pos_q - (WIN - 1))) & (pos_k <= pos_q)
    return jnp.where(allowed, scores, -1e30)


def forward_kernel(
    heads, tile, span, kv_ref, packed_ref, low_ref, chunk_ref,
    query_ref, att_ref, top_ref, inv_ref, att_out, chunk_out, att_packed,
    att_send, att_recv, chunk_send, chunk_recv, own_sems,
):
    size = lax.axis_size("seq")
    first_owner = (size - heads) // 2
    me = lax.axis_index("seq")
    owner = (me >= first_owner) & (me < first_owner + heads)
    barrier = pltpu.get_barrier_semaphore()
    for step in range(1, size):
        pl.semaphore_signal(
            barrier,
            inc=1,
            device_id={"seq": lax.rem(me + step, size)},
            device_id_type=pl.DeviceIdType.MESH,
        )
    pl.semaphore_wait(barrier, size - 1)

    def remote(piece, slot, send_sem, recv_sem, peer):
        return pltpu.make_async_remote_copy(
            src_ref=piece,
            dst_ref=slot,
            send_sem=send_sem,
            recv_sem=recv_sem,
            device_id={"seq": peer},
            device_id_type=pl.DeviceIdType.MESH,
        )

    chunk_copies = []
    for step in range(1, size):
        peer = lax.rem(me + step, size)
        chunk_copies.append(
            remote(
                chunk_ref.at[peer], chunk_out.at[me], chunk_send.at[step], chunk_recv.at[step], peer
            )
        )
    chunk_copies.append(
        pltpu.make_async_copy(chunk_ref.at[me], chunk_out.at[me], own_sems.at[0])
    )
    for copy in chunk_copies:
        copy.start()

    att_slot = att_out.at[jnp.clip(me - first_owner, 0, heads - 1)]

    def att_copy(block, origin):
        return remote(
            att_packed.at[block], att_slot, att_send.at[block], att_recv.at[origin], block
        )

    def own_copy(block):
        return pltpu.make_async_copy(att_packed.at[block], att_slot, own_sems.at[1])

    def run():
        unpack(packed_ref, query_ref, False)
        high_half = lax.broadcasted_iota(jnp.int32, (tile, LANES), 1) >= HEAD

        def query_step(i, _):
            here = pl.ds(pl.multiple_of(i * tile, tile), tile)
            query = query_ref[here, :]
            lowest = low_ref[0:1, here]

            def key_step(j, carry):
                top, total, acc = carry
                kv = kv_ref[pl.ds(pl.multiple_of(j * span, span), span), :]
                scores = masked_scores(kv, query, lowest, j * span, i * tile)
                new_top = jnp.maximum(top, jnp.max(scores, axis=0, keepdims=True))
                raised = jnp.exp(scores - new_top)
                shrink = jnp.exp(top - new_top)
                total = total * shrink + jnp.sum(raised, axis=0, keepdims=True)
                acc = acc * shrink + times_cols(kv, raised.astype(jnp.bfloat16))
                return new_top, total, acc

            start = (
                jnp.full((1, tile), -1e30, jnp.float32),
                jnp.zeros((1, tile), jnp.float32),
                jnp.zeros((LANES, tile), jnp.float32),
            )
            top, total, acc = lax.fori_loop(0, (i * tile + tile - 1) // span + 1, key_step, start)
            inverse = 1.0 / total
            top_ref[0:1, here] = top
            inv_ref[0:1, here] = inverse
            attended = (acc * inverse).T.astype(jnp.bfloat16)
            att_ref[here, :] = jnp.where(high_half, attended, jnp.zeros_like(attended))
            return 0

        tiles = kv_ref.shape[0] // tile
        rows = kv_ref.shape[0] // size
        done = 0
        for stop in range(span // tile, tiles + 1, span // tile):
            lax.fori_loop(stop - span // tile, stop, query_step, 0)
            ready = stop * tile // rows
            pack(att_ref, att_packed, True, range(done, ready))
            for block in range(done, ready):
                pl.when(me != block)(att_copy(block, me).start)
                pl.when(me == block)(own_copy(block).start)
            done = ready
        for block in range(size):
            pl.when(me != block)(att_copy(block, me).wait_send)
            pl.when(me == block)(own_copy(block).wait)

    pl.when(owner)(run)
    for origin in range(first_owner, first_owner + heads):
        pl.when(me != origin)(att_copy(0, origin).wait_recv)
    for copy in chunk_copies:
        copy.wait()


def forward(collective, heads, tile, span, kv, packed_query, low, d_chunk):
    whole, anywhere = pl.BlockSpec(memory_space=pltpu.VMEM), pl.BlockSpec(memory_space=pl.ANY)
    size = lax.axis_size("seq")
    total = kv.shape[0]
    flat = jax.ShapeDtypeStruct(kv.shape, jnp.bfloat16)
    line = jax.ShapeDtypeStruct((1, total), jnp.float32)
    half = packed_query.shape[1]
    sems = pltpu.SemaphoreType.DMA((size,))
    return pl.pallas_call(
        functools.partial(forward_kernel, heads, tile, span),
        out_shape=[
            flat, flat, line, line,
            jax.ShapeDtypeStruct((heads, half, LANES), jnp.bfloat16),
            jax.ShapeDtypeStruct(d_chunk.shape, d_chunk.dtype),
        ],
        in_specs=[whole, whole, whole, anywhere],
        out_specs=[whole] * 4 + [anywhere] * 2,
        scratch_shapes=[
            pltpu.VMEM((size, half, LANES), jnp.bfloat16),
            sems, sems, sems, sems,
            pltpu.SemaphoreType.DMA((2,)),
        ],
        compiler_params=pltpu.CompilerParams(
            collective_id=collective, has_side_effects=True, vmem_limit_bytes=32 * 1024 * 1024
        ),
    )(kv, packed_query, low, d_chunk)


def backward_kernel(
    heads, tile, span, kv_ref, query_ref, packed_ref, low_ref, att_ref, top_ref, inv_ref,
    dq_out, dkv_out, d_att_ref, dq_ref, d_kv,
):
    def run():
        unpack(packed_ref, d_att_ref, True)
        d_kv[...] = jnp.zeros_like(d_kv)

        def query_step(i, _):
            here = pl.ds(pl.multiple_of(i * tile, tile), tile)
            query, d_att = query_ref[here, :], d_att_ref[here, :]
            lowest, top, inverse = low_ref[0:1, here], top_ref[0:1, here], inv_ref[0:1, here]
            product = att_ref[here, :].astype(jnp.float32) * d_att.astype(jnp.float32)
            delta = jnp.sum(product.T, axis=0, keepdims=True)

            def key_step(j, acc):
                there = pl.ds(pl.multiple_of(j * span, span), span)
                kv = kv_ref[there, :]
                scores = masked_scores(kv, query, lowest, j * span, i * tile)
                probs = jnp.exp(scores - top) * inverse
                d_probs = times_rows(kv, d_att)
                d_scores = (probs * (d_probs - delta)).astype(jnp.bfloat16)
                d_kv[there, :] += jnp.dot(
                    d_scores, query, preferred_element_type=jnp.float32
                ) + jnp.dot(
                    probs.astype(jnp.bfloat16), d_att, preferred_element_type=jnp.float32
                )
                return acc + times_cols(kv, d_scores)

            zero = jnp.zeros((LANES, tile), jnp.float32)
            acc = lax.fori_loop(0, (i * tile + tile - 1) // span + 1, key_step, zero)
            dq_ref[here, :] = (acc * HEAD ** (-0.5)).T.astype(jnp.bfloat16)
            return 0

        lax.fori_loop(0, kv_ref.shape[0] // tile, query_step, 0)
        dkv_out[...] = d_kv[...].astype(jnp.bfloat16)
        pack(dq_ref, dq_out, False)

    when_owner(heads, run)


def tiling(total):
    tile = next(size for size in (256, 128) if total % size == 0)
    return tile, tile * (3 if total % (3 * tile) == 0 else 1)


def plain_call(body, arrays, shapes, scratch=()):
    whole = pl.BlockSpec(memory_space=pltpu.VMEM)
    return pl.pallas_call(
        body,
        out_shape=[jax.ShapeDtypeStruct(*shape) for shape in shapes],
        in_specs=[whole] * len(arrays),
        out_specs=[whole] * len(shapes),
        scratch_shapes=list(scratch),
        compiler_params=pltpu.CompilerParams(vmem_limit_bytes=32 * 1024 * 1024),
    )(*arrays)


def twist(left, right):
    low_half = lax.broadcasted_iota(jnp.int32, left.shape, 1) < HEAD
    first = jnp.where(low_half, left, rolled(right).astype(left.dtype))
    second = jnp.where(low_half, rolled(left).astype(left.dtype), right)
    return first, second


def split_pairs(left, right, out_ref):
    for pair in range(left.shape[1] // LANES):
        lanes = slice(pair * LANES, (pair + 1) * LANES)
        out_ref[2 * pair], out_ref[2 * pair + 1] = twist(left[:, lanes], right[:, lanes])


def join_pairs(ref):
    lefts, rights = zip(*(twist(ref[head], ref[head + 1]) for head in range(0, ref.shape[0], 2)))
    return jnp.concatenate(lefts, axis=1), jnp.concatenate(rights, axis=1)


def rounded_dot(left, right):
    return jnp.dot(left, right, preferred_element_type=jnp.float32).astype(jnp.bfloat16)


def prepare_kernel(x_ref, gain_ref, wq_ref, wk_ref, wv_ref, kv_ref, packed_ref):
    x = x_ref[...].astype(jnp.float32)
    scale_r = lax.rsqrt(jnp.mean(x * x, axis=-1, keepdims=True) + 1e-05)
    normed = (x * scale_r * gain_ref[...]).astype(jnp.bfloat16)
    split_pairs(rounded_dot(normed, wk_ref[...]), rounded_dot(normed, wv_ref[...]), kv_ref)
    query = rounded_dot(normed, wq_ref[...]) * jnp.bfloat16(HEAD ** (-0.5))
    half = query.shape[0] // 2
    split_pairs(query[:half], query[half:], packed_ref)


def project_kernel(parts, packed_ref, w_ref, x_ref, out_ref):
    top, bottom = join_pairs(packed_ref)
    half = top.shape[0]
    for rows, part in ((slice(0, half), top), (slice(half, 2 * half), bottom)):
        product = jnp.dot(part, w_ref[...], preferred_element_type=jnp.float32)
        x = x_ref[rows, :].astype(jnp.float32) * (1.0 / parts)
        out_ref[rows, :] = (product + x).astype(jnp.bfloat16)


def d_attended_kernel(d_mixed_ref, w_ref, packed_ref):
    d_attended = times_rows(d_mixed_ref[...], w_ref[...]).astype(jnp.bfloat16)
    half = d_attended.shape[0] // 2
    split_pairs(d_attended[:half], d_attended[half:], packed_ref)


def d_normed_kernel(dq_ref, dkv_ref, wq_ref, wk_ref, wv_ref, out_ref):
    d_query = jnp.concatenate(join_pairs(dq_ref), axis=0)
    d_key, d_value = join_pairs(dkv_ref)
    total = times_rows(d_query, wq_ref[...]) + times_rows(d_key, wk_ref[...])
    out_ref[...] = (total + times_rows(d_value, wv_ref[...])).astype(jnp.bfloat16)


def by_head_owner(
    tokens, norm_gain, w_query, w_key, w_value, w_out, w_shorten, first_key, d_faces
):
    tok_rows, model_width = tokens.shape
    face_rows = tok_rows // 9
    width = w_query.shape[1]
    heads = width // HEAD
    seq_count, mp_count = lax.axis_size("seq"), lax.axis_size("mp")
    share = face_rows // mp_count
    halves = 16 // share
    chunk = w_shorten.shape[0] // halves
    padded = -(-chunk // 128) * 128
    tok_total = tok_rows * seq_count
    faces_total = face_rows * seq_count
    bf16, f32 = jnp.bfloat16, jnp.float32

    wide = -(-face_rows // 128) * 128
    bounds = jnp.broadcast_to(jnp.pad(first_key, (0, wide - face_rows))[None], (8, wide))
    all_d_faces, all_bounds = exchange(
        1, [(d_faces, "seq", "same"), (bounds, "seq", "same")]
    )
    low = jnp.repeat(all_bounds[:, 0, :face_rows].reshape(faces_total), 9)[None]

    shorten = jnp.pad(
        w_shorten.reshape(halves, chunk, -1), ((0, 0), (0, padded - chunk), (0, 0))
    )
    by_share = all_d_faces.reshape(seq_count, mp_count, share, -1).transpose(1, 0, 2, 3)
    by_share = by_share.reshape(faces_total, -1)
    d_partial = [
        times_rows(by_share, shorten[half])
        .astype(bf16)
        .reshape(mp_count, seq_count, share, padded)
        for half in range(halves)
    ]
    d_partial = jnp.concatenate(d_partial, axis=2)
    d_partial = d_partial.reshape(mp_count, seq_count * halves * share, padded)

    half_rows = tok_rows // 2
    kv, packed_query = plain_call(
        prepare_kernel,
        (tokens, norm_gain[None], w_query, w_key, w_value),
        (((heads, tok_rows, LANES), bf16), ((heads, half_rows, LANES), bf16)),
    )
    kv, packed_query, d_chunk = exchange(
        2,
        [
            (kv, "seq", "to_heads"),
            (packed_query, "seq", "to_heads"),
            (d_partial, "mp", "reduce"),
        ],
        heads,
    )
    kv = kv.reshape(tok_total, LANES)
    tile, span = tiling(tok_total)
    flat = ((tok_total, LANES), bf16)
    folded = ((seq_count, half_rows, LANES), bf16)
    moved = (seq_count, halves * share, padded)
    query_flat, att_flat, top, inverse, att_packed, d_chunk = forward(
        3, heads, tile, span, kv, packed_query, low, d_chunk.reshape(moved)
    )
    (projected,) = plain_call(
        functools.partial(project_kernel, mp_count),
        (att_packed, w_out, tokens),
        [((tok_rows, model_width), bf16)],
    )
    d_chunk = d_chunk.reshape(seq_count, halves, share, padded)[..., :chunk]
    d_chunk = d_chunk.transpose(2, 0, 1, 3).reshape(tok_rows // mp_count, model_width)
    d_mixed, mixed = exchange(
        4,
        [
            (d_chunk, "mp", "gather"),
            (projected.reshape(mp_count, *d_chunk.shape), "mp", "reduce"),
        ],
    )
    d_mixed = d_mixed.reshape(tok_rows, model_width)
    (d_att_packed,) = plain_call(
        d_attended_kernel, (d_mixed, w_out), [((heads, half_rows, LANES), bf16)]
    )
    mixed = mixed.reshape(share, seq_count, halves, chunk).transpose(1, 2, 0, 3)
    mixed = jnp.pad(mixed, ((0, 0), (0, 0), (0, 0), (0, padded - chunk))).reshape(moved)
    d_att_packed, mixed = exchange(
        5, [(d_att_packed, "seq", "to_heads"), (mixed, "seq", "all")], heads
    )
    d_query, d_kv = plain_call(
        functools.partial(backward_kernel, heads, tile, span),
        (kv, query_flat, d_att_packed, low, att_flat, top, inverse),
        (folded, flat),
        [pltpu.VMEM(*flat), pltpu.VMEM(*flat), pltpu.VMEM(flat[0], f32)],
    )
    d_query, d_kv, mixed = exchange(
        6,
        [
            (d_query, "seq", "from_heads"),
            (d_kv.reshape(seq_count, tok_rows, LANES), "seq", "from_heads"),
            (mixed, "mp", "gather"),
        ],
        heads,
    )
    (part_normed,) = plain_call(
        d_normed_kernel,
        (d_query, d_kv, w_query, w_key, w_value),
        [((tok_rows, model_width), bf16)],
    )
    mixed = mixed.reshape(mp_count, seq_count, halves, share, padded)
    partial = sum(
        jnp.dot(
            mixed[:, :, half].reshape(faces_total, padded),
            shorten[half],
            preferred_element_type=f32,
        )
        for half in range(halves)
    )
    partial = partial.astype(bf16).reshape(mp_count, seq_count, share, -1)
    partial = partial.transpose(1, 0, 2, 3).reshape(seq_count, face_rows, -1)
    part_normed, partial = exchange(
        7,
        [
            (part_normed.reshape(mp_count, *d_chunk.shape), "mp", "reduce"),
            (partial, "seq", "all"),
        ],
    )
    (d_normed,) = exchange(8, [(part_normed, "mp", "gather")])
    faces = jnp.sum(partial.astype(f32), axis=0).astype(bf16)
    d_normed = d_normed.reshape(tok_rows, model_width).astype(f32)
    x_float = tokens.astype(f32)
    scale_r = lax.rsqrt(jnp.mean(x_float * x_float, axis=-1, keepdims=True) + 1e-05)
    d_tokens = finish(d_normed, x_float, scale_r, d_mixed, norm_gain).astype(bf16)
    return (faces, d_tokens)


def by_window(tokens, norm_gain, w_query, w_key, w_value, w_out, w_shorten, first_key, d_faces):
    tok_rows = tokens.shape[0]
    model_width = tokens.shape[1]
    face_rows = tok_rows // 9
    local_width = w_query.shape[1]
    local_heads = local_width // HEAD
    seq_count = lax.axis_size("seq")
    hops = min(-(-WIN // tok_rows), seq_count - 1)
    levels = hops.bit_length()
    seq_index = lax.axis_index("seq")
    x_float = tokens.astype(jnp.float32)
    scale_r = lax.rsqrt(jnp.mean(x_float * x_float, axis=-1, keepdims=True) + 1e-05)
    normed = (x_float * scale_r * norm_gain).astype(jnp.bfloat16)
    query = jnp.dot(normed, w_query, preferred_element_type=jnp.float32).astype(jnp.bfloat16)
    key = jnp.dot(normed, w_key, preferred_element_type=jnp.float32).astype(jnp.bfloat16)
    value = jnp.dot(normed, w_value, preferred_element_type=jnp.float32).astype(jnp.bfloat16)
    stacked_key = key[None]
    stacked_value = value[None]
    for level in range(levels):
        reach_by = 1 << level
        came_key, came_value = shifted((stacked_key, stacked_value), "seq", reach_by)
        stacked_key = jnp.concatenate([stacked_key, came_key], axis=0)
        stacked_value = jnp.concatenate([stacked_value, came_value], axis=0)
    anchors = seq_index - jnp.arange(hops + 1, dtype=jnp.int32)
    block_count = stacked_key.shape[0]
    key_total = block_count * tok_rows
    pos_q = seq_index * tok_rows + jnp.arange(tok_rows, dtype=jnp.int32)
    pos_k = (anchors[:, None] * tok_rows + jnp.arange(tok_rows, dtype=jnp.int32)[None, :]).reshape(
        key_total
    )
    lower_bound = jnp.repeat(first_key, 9)
    allowed = (
        (pos_k[None, :] >= lower_bound[:, None])
        & (pos_k[None, :] <= pos_q[:, None])
        & (pos_q[:, None] - pos_k[None, :] < WIN)
    )
    query_heads = query.reshape(tok_rows, local_heads, HEAD).transpose(1, 0, 2)
    key_heads = stacked_key.reshape(key_total, local_heads, HEAD).transpose(1, 0, 2)
    value_heads = stacked_value.reshape(key_total, local_heads, HEAD).transpose(1, 0, 2)

    def head_probs(query_head, key_head):
        scores = times_rows(query_head, key_head) * HEAD ** (-0.5)
        scores = jnp.where(allowed, scores, -1e30)
        row_top = jnp.max(scores, axis=-1, keepdims=True)
        raised = jnp.exp(scores - row_top)
        return raised / jnp.sum(raised, axis=-1, keepdims=True)

    def head_forward(operands):
        query_head, key_head, value_head = operands
        probs = head_probs(query_head, key_head)
        return jnp.dot(
            probs.astype(jnp.bfloat16), value_head, preferred_element_type=jnp.float32
        ).astype(jnp.bfloat16)

    att_heads = lax.map(head_forward, (query_heads, key_heads, value_heads))
    attended = att_heads.transpose(1, 0, 2).reshape(tok_rows, local_width)
    projected = jnp.dot(attended, w_out, preferred_element_type=jnp.float32)
    summed = lax.psum(projected.astype(jnp.bfloat16), "mp").astype(jnp.float32)
    mixed = (x_float + summed).astype(jnp.bfloat16)
    mixed_faces = mixed.reshape(face_rows, 9 * model_width)
    full_shorten = lax.all_gather(w_shorten, "seq", axis=0, tiled=True)
    face_sum = jnp.dot(mixed_faces, full_shorten, preferred_element_type=jnp.float32)
    d_partial = times_rows(d_faces, full_shorten)
    faces = face_sum.astype(jnp.bfloat16)
    d_mixed = lax.psum(d_partial, "mp").astype(jnp.bfloat16).reshape(tok_rows, model_width)
    d_attended = times_rows(d_mixed, w_out).astype(jnp.bfloat16)
    d_att_heads = d_attended.reshape(tok_rows, local_heads, HEAD).transpose(1, 0, 2)

    def head_backward(operands):
        query_head, key_head, value_head, d_att_head, att_head = operands
        probs = head_probs(query_head, key_head)
        d_probs = times_rows(d_att_head, value_head)
        row_delta = jnp.sum(d_att_head.astype(jnp.float32) * att_head.astype(jnp.float32), axis=-1)
        d_scores = (probs * (d_probs - row_delta[:, None])).astype(jnp.bfloat16)
        d_query_head = (
            jnp.dot(d_scores, key_head, preferred_element_type=jnp.float32) * HEAD ** (-0.5)
        ).astype(jnp.bfloat16)
        d_key_head = times_cols(d_scores, query_head) * HEAD ** (-0.5)
        d_value_head = times_cols(probs.astype(jnp.bfloat16), d_att_head)
        return (d_query_head, d_key_head, d_value_head)

    d_query_heads, d_key_heads, d_value_heads = lax.map(
        head_backward, (query_heads, key_heads, value_heads, d_att_heads, att_heads)
    )
    d_query = d_query_heads.transpose(1, 0, 2).reshape(tok_rows, local_width)
    d_key_parts = d_key_heads.transpose(1, 0, 2).reshape(block_count, tok_rows, local_width)
    d_value_parts = d_value_heads.transpose(1, 0, 2).reshape(block_count, tok_rows, local_width)
    spare_blocks = (1 << levels) - block_count
    filler = jnp.zeros((spare_blocks, tok_rows, local_width), jnp.float32)
    parts_key = jnp.concatenate([d_key_parts, filler], axis=0)
    parts_value = jnp.concatenate([d_value_parts, filler], axis=0)
    for level in reversed(range(levels)):
        reach_by = 1 << level
        came_key, came_value = shifted(
            (
                shortened(parts_key[reach_by : 2 * reach_by]),
                shortened(parts_value[reach_by : 2 * reach_by]),
            ),
            "seq",
            -reach_by,
        )
        parts_key = parts_key[:reach_by] + came_key
        parts_value = parts_value[:reach_by] + came_value
    acc_key, acc_value = (parts_key[0], parts_value[0])
    d_key = acc_key.astype(jnp.bfloat16)
    d_value = acc_value.astype(jnp.bfloat16)
    part_normed = times_rows(d_query, w_query)
    part_normed = part_normed + times_rows(d_key, w_key)
    part_normed = part_normed + times_rows(d_value, w_value)
    d_normed = lax.psum(part_normed.astype(jnp.bfloat16), "mp").astype(jnp.float32)
    d_tokens = finish(d_normed, x_float, scale_r, d_mixed, norm_gain).astype(jnp.bfloat16)
    return (faces, d_tokens)


def local(*arrays):
    heads = arrays[2].shape[1] // HEAD
    seq_count = lax.axis_size("seq")
    whole_pairs = heads % 2 == 0 and lax.axis_size("mp") == 4
    if heads <= seq_count < 2 * heads and whole_pairs:
        return by_head_owner(*arrays)
    return by_window(*arrays)


def solution(mesh):
    in_specs = (
        P("seq", None),
        P(),
        P(None, "mp"),
        P(None, "mp"),
        P(None, "mp"),
        P("mp", None),
        P("seq", "mp"),
        P("seq"),
        P("seq", "mp"),
    )
    out_specs = (P("seq", "mp"), P("seq", None))
    return jax.shard_map(local, mesh=mesh, in_specs=in_specs, out_specs=out_specs, check_vma=False)
```

```python
import functools

import jax
import jax.numpy as jnp
from jax import lax
from jax.experimental import pallas as pl
from jax.experimental.pallas import tpu as pltpu
from jax.sharding import PartitionSpec as P

HEAD = 64
WIN = 4096
LANES = 2 * HEAD


def shifted(array, axis, by):
    size = lax.axis_size(axis)
    pairs = [(i, i + by) for i in range(size) if 0 <= i + by < size]
    return lax.ppermute(array, axis, pairs)


def shortened(array):

    def short(part):
        return part.astype(jnp.bfloat16) if part.dtype == jnp.float32 else part

    return jax.tree.map(short, array)


def times_rows(left, right):
    return lax.dot_general(
        left, right, (((1,), (1,)), ((), ())), preferred_element_type=jnp.float32
    )


def times_cols(left, right):
    return lax.dot_general(
        left, right, (((0,), (0,)), ((), ())), preferred_element_type=jnp.float32
    )


def finish(d_normed, x_float, scale_r, d_mixed, norm_gain):
    inner_sum = jnp.mean(d_normed * norm_gain * x_float, axis=-1, keepdims=True)
    return (
        d_mixed.astype(jnp.float32)
        + scale_r * norm_gain * d_normed
        - x_float * scale_r**3 * inner_sum
    )


def exchange_kernel(plan, heads, first_owner, *refs):
    count = len(plan)
    sources, targets = refs[:count], refs[count : 2 * count]
    send_sems, recv_sems, own_sem = refs[2 * count : 2 * count + 3]
    spares = refs[2 * count + 3 :]
    barrier = pltpu.get_barrier_semaphore()
    greeted = 0
    for axis in sorted({axis for axis, _ in plan}):
        size = lax.axis_size(axis)
        for step in range(1, size):
            peer = lax.rem(lax.axis_index(axis) + step, size)
            pl.semaphore_signal(
                barrier, inc=1, device_id={axis: peer}, device_id_type=pl.DeviceIdType.MESH
            )
            greeted += 1
    pl.semaphore_wait(barrier, greeted)

    def owns(place):
        return (place >= first_owner) & (place < first_owner + heads)

    def when(condition, action):
        if condition is None:
            action()
        else:
            pl.when(condition)(action)

    def remote(item, step, piece, slot, axis, peer):
        return pltpu.make_async_remote_copy(
            src_ref=piece,
            dst_ref=slot,
            send_sem=send_sems.at[item, step],
            recv_sem=recv_sems.at[item, step],
            device_id={axis: peer},
            device_id_type=pl.DeviceIdType.MESH,
        )

    finals = []
    paired = []
    for item, (axis, kind) in sorted(enumerate(plan), key=lambda pair: pair[1][1] not in PAIRED):
        source, target = sources[item], targets[item]
        size = lax.axis_size(axis)
        me = lax.axis_index(axis)
        if kind in PAIRED:
            near = me + 1 - 2 * lax.rem(me, 2)
            far = lax.rem(me + 2, 4)
            far_near = lax.rem(near + 2, 4)
            link = functools.partial(remote, item)
            if kind == "gather":
                own = pltpu.make_async_copy(source, target.at[me], own_sem.at[item])
                own.start()
                first = [
                    link(0, source, target.at[me], axis, far),
                    link(1, source, target.at[me], axis, near),
                ]
                second = link(2, target.at[far], target.at[far], axis, near)
            else:
                came, joined, crossed = spares[:3]
                spares = spares[3:]
                first = [
                    link(0, source.at[far_near], came.at[0], axis, near),
                    link(1, source.at[near], came.at[1], axis, near),
                ]
                second = link(2, joined, crossed, axis, far)
                own = None
            for copy in first:
                copy.start()
            paired.append((item, kind, me, far, first, second, own))
            if kind == "reduce":
                paired[-1] += (came, joined, crossed)
            continue
        for step in list(range(1, size)) + [0]:
            peer = lax.rem(me + step, size)
            origin = lax.rem(me + size - step, size)
            send_if = recv_if = None
            if kind == "all":
                piece, slot = source.at[peer], target.at[me]
            elif kind == "same":
                piece, slot = source, target.at[me]
            elif kind == "to_heads":
                piece = source.at[jnp.clip(peer - first_owner, 0, heads - 1)]
                slot = target.at[me]
                send_if, recv_if = owns(peer), owns(me)
            else:
                piece = source.at[peer]
                slot = target.at[jnp.clip(me - first_owner, 0, heads - 1)]
                send_if, recv_if = owns(me), owns(origin)
            if step == 0:
                copy = pltpu.make_async_copy(piece, slot, own_sem.at[item])
                when(send_if, copy.start)
                finals.append((send_if, copy.wait))
            else:
                copy = remote(item, step, piece, slot, axis, peer)
                when(send_if, copy.start)
                finals.append((send_if, copy.wait_send))
                finals.append((recv_if, copy.wait_recv))

    def added(left, right):
        return (left.astype(jnp.float32) + right.astype(jnp.float32)).astype(jnp.bfloat16)

    for item, kind, me, far, first, second, own, *held in paired:
        if kind == "gather":
            first[0].wait_recv()
            second.start()
        else:
            came, joined, crossed = held
            first[0].wait_recv()
            joined[...] = added(sources[item][far], came[0])
            second.start()
    for item, kind, me, far, first, second, own, *held in paired:
        if kind == "gather":
            first[0].wait_send()
            first[1].wait()
            second.wait()
            own.wait()
        else:
            came, joined, crossed = held
            first[1].wait_recv()
            mine = sources[item][me].astype(jnp.float32) + came[1].astype(jnp.float32)
            second.wait_recv()
            targets[item][...] = (mine + crossed[...].astype(jnp.float32)).astype(jnp.bfloat16)
            first[0].wait_send()
            first[1].wait_send()
            second.wait_send()
    for condition, action in finals:
        when(condition, action)


PAIRED = ("gather", "reduce")


def exchange(collective, items, heads=1):
    plan, shapes, spares, in_specs, out_specs = [], [], [], [], []
    most = 3
    for array, axis, kind in items:
        size = lax.axis_size(axis)
        most = max(most, size)
        plan.append((axis, kind))
        tail = array.shape if kind in ("same", "gather") else array.shape[1:]
        lead = heads if kind == "from_heads" else size
        space = pl.ANY
        if kind == "reduce":
            shapes.append(jax.ShapeDtypeStruct(tail, array.dtype))
            spares.append(pltpu.VMEM((2, *tail), array.dtype))
            spares += [pltpu.VMEM(tail, array.dtype)] * 2
            space = pltpu.VMEM
        else:
            shapes.append(jax.ShapeDtypeStruct((lead, *tail), array.dtype))
        in_specs.append(pl.BlockSpec(memory_space=space))
        out_specs.append(pl.BlockSpec(memory_space=space))
    first_owner = (lax.axis_size("seq") - heads) // 2
    return pl.pallas_call(
        functools.partial(exchange_kernel, tuple(plan), heads, first_owner),
        out_shape=shapes,
        in_specs=in_specs,
        out_specs=out_specs,
        scratch_shapes=[
            pltpu.SemaphoreType.DMA((len(plan), most)),
            pltpu.SemaphoreType.DMA((len(plan), most)),
            pltpu.SemaphoreType.DMA((len(plan),)),
            *spares,
        ],
        compiler_params=pltpu.CompilerParams(
            collective_id=collective, has_side_effects=True, vmem_limit_bytes=24 * 1024 * 1024
        ),
    )(*[array for array, _, _ in items])


def when_owner(heads, action):
    first_owner = (lax.axis_size("seq") - heads) // 2
    me = lax.axis_index("seq")
    pl.when((me >= first_owner) & (me < first_owner + heads))(action)


def rolled(array):
    return pltpu.roll(array.astype(jnp.float32), HEAD, 1)


def unpack(packed_ref, flat_ref, upper):
    blocks, half, _ = packed_ref.shape
    low_half = lax.broadcasted_iota(jnp.int32, (half, LANES), 1) < HEAD
    for block in range(blocks):
        packed = packed_ref[block]
        other = rolled(packed).astype(packed.dtype)
        parts = (other, packed) if upper else (packed, other)
        zero = jnp.zeros_like(packed)
        for place, part in enumerate(parts):
            part = jnp.where(low_half, zero, part) if upper else jnp.where(low_half, part, zero)
            flat_ref[pl.ds((2 * block + place) * half, half), :] = part


def pack(flat_ref, packed_ref, upper, chosen=None):
    blocks, half, _ = packed_ref.shape
    low_half = lax.broadcasted_iota(jnp.int32, (half, LANES), 1) < HEAD
    for block in range(blocks) if chosen is None else chosen:
        top = flat_ref[pl.ds(2 * block * half, half), :]
        bottom = flat_ref[pl.ds((2 * block + 1) * half, half), :]
        if upper:
            top = rolled(top).astype(top.dtype)
        else:
            bottom = rolled(bottom).astype(top.dtype)
        packed_ref[block] = jnp.where(low_half, top, bottom)


def masked_scores(kv, query, lowest, key_start, query_start):
    scores = times_rows(kv, query)
    pos_k = key_start + lax.broadcasted_iota(jnp.int32, scores.shape, 0)
    pos_q = query_start + lax.broadcasted_iota(jnp.int32, (1, scores.shape[1]), 1)
    allowed = (pos_k >= jnp.maximum(lowest, pos_q - (WIN - 1))) & (pos_k <= pos_q)
    return jnp.where(allowed, scores, -1e30)


def forward_kernel(
    heads, tile, span, kv_ref, packed_ref, low_ref, chunk_ref,
    query_ref, att_ref, top_ref, inv_ref, att_out, chunk_out, att_packed,
    att_send, att_recv, chunk_send, chunk_recv, own_sems,
):
    size = lax.axis_size("seq")
    first_owner = (size - heads) // 2
    me = lax.axis_index("seq")
    owner = (me >= first_owner) & (me < first_owner + heads)
    barrier = pltpu.get_barrier_semaphore()
    for step in range(1, size):
        pl.semaphore_signal(
            barrier,
            inc=1,
            device_id={"seq": lax.rem(me + step, size)},
            device_id_type=pl.DeviceIdType.MESH,
        )
    pl.semaphore_wait(barrier, size - 1)

    def remote(piece, slot, send_sem, recv_sem, peer):
        return pltpu.make_async_remote_copy(
            src_ref=piece,
            dst_ref=slot,
            send_sem=send_sem,
            recv_sem=recv_sem,
            device_id={"seq": peer},
            device_id_type=pl.DeviceIdType.MESH,
        )

    chunk_copies = []
    for step in range(1, size):
        peer = lax.rem(me + step, size)
        chunk_copies.append(
            remote(
                chunk_ref.at[peer], chunk_out.at[me], chunk_send.at[step], chunk_recv.at[step], peer
            )
        )
    chunk_copies.append(
        pltpu.make_async_copy(chunk_ref.at[me], chunk_out.at[me], own_sems.at[0])
    )
    for copy in chunk_copies:
        copy.start()

    att_slot = att_out.at[jnp.clip(me - first_owner, 0, heads - 1)]

    def att_copy(block, origin):
        return remote(
            att_packed.at[block], att_slot, att_send.at[block], att_recv.at[origin], block
        )

    def own_copy(block):
        return pltpu.make_async_copy(att_packed.at[block], att_slot, own_sems.at[1])

    def run():
        unpack(packed_ref, query_ref, False)
        high_half = lax.broadcasted_iota(jnp.int32, (tile, LANES), 1) >= HEAD

        def query_step(i, _):
            here = pl.ds(pl.multiple_of(i * tile, tile), tile)
            query = query_ref[here, :]
            lowest = low_ref[0:1, here]

            def key_step(j, carry):
                top, total, acc = carry
                kv = kv_ref[pl.ds(pl.multiple_of(j * span, span), span), :]
                scores = masked_scores(kv, query, lowest, j * span, i * tile)
                new_top = jnp.maximum(top, jnp.max(scores, axis=0, keepdims=True))
                raised = jnp.exp(scores - new_top)
                shrink = jnp.exp(top - new_top)
                total = total * shrink + jnp.sum(raised, axis=0, keepdims=True)
                acc = acc * shrink + times_cols(kv, raised.astype(jnp.bfloat16))
                return new_top, total, acc

            start = (
                jnp.full((1, tile), -1e30, jnp.float32),
                jnp.zeros((1, tile), jnp.float32),
                jnp.zeros((LANES, tile), jnp.float32),
            )
            top, total, acc = lax.fori_loop(0, (i * tile + tile - 1) // span + 1, key_step, start)
            inverse = 1.0 / total
            top_ref[0:1, here] = top
            inv_ref[0:1, here] = inverse
            attended = (acc * inverse).T.astype(jnp.bfloat16)
            att_ref[here, :] = jnp.where(high_half, attended, jnp.zeros_like(attended))
            return 0

        tiles = kv_ref.shape[0] // tile
        rows = kv_ref.shape[0] // size
        done = 0
        for stop in range(span // tile, tiles + 1, span // tile):
            lax.fori_loop(stop - span // tile, stop, query_step, 0)
            ready = stop * tile // rows
            pack(att_ref, att_packed, True, range(done, ready))
            for block in range(done, ready):
                pl.when(me != block)(att_copy(block, me).start)
                pl.when(me == block)(own_copy(block).start)
            done = ready
        for block in range(size):
            pl.when(me != block)(att_copy(block, me).wait_send)
            pl.when(me == block)(own_copy(block).wait)

    pl.when(owner)(run)
    for origin in range(first_owner, first_owner + heads):
        pl.when(me != origin)(att_copy(0, origin).wait_recv)
    for copy in chunk_copies:
        copy.wait()


def forward(collective, heads, tile, span, kv, packed_query, low, d_chunk):
    whole, anywhere = pl.BlockSpec(memory_space=pltpu.VMEM), pl.BlockSpec(memory_space=pl.ANY)
    size = lax.axis_size("seq")
    total = kv.shape[0]
    flat = jax.ShapeDtypeStruct(kv.shape, jnp.bfloat16)
    line = jax.ShapeDtypeStruct((1, total), jnp.float32)
    half = packed_query.shape[1]
    sems = pltpu.SemaphoreType.DMA((size,))
    return pl.pallas_call(
        functools.partial(forward_kernel, heads, tile, span),
        out_shape=[
            flat, flat, line, line,
            jax.ShapeDtypeStruct((heads, half, LANES), jnp.bfloat16),
            jax.ShapeDtypeStruct(d_chunk.shape, d_chunk.dtype),
        ],
        in_specs=[whole, whole, whole, anywhere],
        out_specs=[whole] * 4 + [anywhere] * 2,
        scratch_shapes=[
            pltpu.VMEM((size, half, LANES), jnp.bfloat16),
            sems, sems, sems, sems,
            pltpu.SemaphoreType.DMA((2,)),
        ],
        compiler_params=pltpu.CompilerParams(
            collective_id=collective, has_side_effects=True, vmem_limit_bytes=32 * 1024 * 1024
        ),
    )(kv, packed_query, low, d_chunk)


def backward_kernel(
    heads, tile, span, kv_ref, query_ref, packed_ref, low_ref, att_ref, top_ref, inv_ref,
    dq_out, dkv_out, d_att_ref, dq_ref, d_kv,
):
    def run():
        unpack(packed_ref, d_att_ref, True)
        d_kv[...] = jnp.zeros_like(d_kv)

        def query_step(i, _):
            here = pl.ds(pl.multiple_of(i * tile, tile), tile)
            query, d_att = query_ref[here, :], d_att_ref[here, :]
            lowest, top, inverse = low_ref[0:1, here], top_ref[0:1, here], inv_ref[0:1, here]
            product = att_ref[here, :].astype(jnp.float32) * d_att.astype(jnp.float32)
            delta = jnp.sum(product.T, axis=0, keepdims=True)

            def key_step(j, acc):
                there = pl.ds(pl.multiple_of(j * span, span), span)
                kv = kv_ref[there, :]
                scores = masked_scores(kv, query, lowest, j * span, i * tile)
                probs = jnp.exp(scores - top) * inverse
                d_probs = times_rows(kv, d_att)
                d_scores = (probs * (d_probs - delta)).astype(jnp.bfloat16)
                d_kv[there, :] += jnp.dot(
                    d_scores, query, preferred_element_type=jnp.float32
                ) + jnp.dot(
                    probs.astype(jnp.bfloat16), d_att, preferred_element_type=jnp.float32
                )
                return acc + times_cols(kv, d_scores)

            zero = jnp.zeros((LANES, tile), jnp.float32)
            acc = lax.fori_loop(0, (i * tile + tile - 1) // span + 1, key_step, zero)
            dq_ref[here, :] = (acc * HEAD ** (-0.5)).T.astype(jnp.bfloat16)
            return 0

        lax.fori_loop(0, kv_ref.shape[0] // tile, query_step, 0)
        dkv_out[...] = d_kv[...].astype(jnp.bfloat16)
        pack(dq_ref, dq_out, False)

    when_owner(heads, run)


def tiling(total):
    tile = next(size for size in (384, 256, 128) if total % size == 0)
    return tile, tile * (2 if total % (2 * tile) == 0 else 1)


def plain_call(body, arrays, shapes, scratch=()):
    whole = pl.BlockSpec(memory_space=pltpu.VMEM)
    return pl.pallas_call(
        body,
        out_shape=[jax.ShapeDtypeStruct(*shape) for shape in shapes],
        in_specs=[whole] * len(arrays),
        out_specs=[whole] * len(shapes),
        scratch_shapes=list(scratch),
        compiler_params=pltpu.CompilerParams(vmem_limit_bytes=32 * 1024 * 1024),
    )(*arrays)


def twist(left, right):
    low_half = lax.broadcasted_iota(jnp.int32, left.shape, 1) < HEAD
    first = jnp.where(low_half, left, rolled(right).astype(left.dtype))
    second = jnp.where(low_half, rolled(left).astype(left.dtype), right)
    return first, second


def split_pairs(left, right, out_ref):
    for pair in range(left.shape[1] // LANES):
        lanes = slice(pair * LANES, (pair + 1) * LANES)
        out_ref[2 * pair], out_ref[2 * pair + 1] = twist(left[:, lanes], right[:, lanes])


def join_pairs(ref):
    lefts, rights = zip(*(twist(ref[head], ref[head + 1]) for head in range(0, ref.shape[0], 2)))
    return jnp.concatenate(lefts, axis=1), jnp.concatenate(rights, axis=1)


def rounded_dot(left, right):
    return jnp.dot(left, right, preferred_element_type=jnp.float32).astype(jnp.bfloat16)


def prepare_kernel(x_ref, gain_ref, wq_ref, wk_ref, wv_ref, kv_ref, packed_ref):
    x = x_ref[...].astype(jnp.float32)
    scale_r = lax.rsqrt(jnp.mean(x * x, axis=-1, keepdims=True) + 1e-05)
    normed = (x * scale_r * gain_ref[...]).astype(jnp.bfloat16)
    split_pairs(rounded_dot(normed, wk_ref[...]), rounded_dot(normed, wv_ref[...]), kv_ref)
    query = rounded_dot(normed, wq_ref[...]) * jnp.bfloat16(HEAD ** (-0.5))
    half = query.shape[0] // 2
    split_pairs(query[:half], query[half:], packed_ref)


def project_kernel(parts, packed_ref, w_ref, x_ref, out_ref):
    top, bottom = join_pairs(packed_ref)
    half = top.shape[0]
    for rows, part in ((slice(0, half), top), (slice(half, 2 * half), bottom)):
        product = jnp.dot(part, w_ref[...], preferred_element_type=jnp.float32)
        x = x_ref[rows, :].astype(jnp.float32) * (1.0 / parts)
        out_ref[rows, :] = (product + x).astype(jnp.bfloat16)


def d_attended_kernel(d_mixed_ref, w_ref, packed_ref):
    d_attended = times_rows(d_mixed_ref[...], w_ref[...]).astype(jnp.bfloat16)
    half = d_attended.shape[0] // 2
    split_pairs(d_attended[:half], d_attended[half:], packed_ref)


def d_normed_kernel(dq_ref, dkv_ref, wq_ref, wk_ref, wv_ref, out_ref):
    d_query = jnp.concatenate(join_pairs(dq_ref), axis=0)
    d_key, d_value = join_pairs(dkv_ref)
    total = times_rows(d_query, wq_ref[...]) + times_rows(d_key, wk_ref[...])
    out_ref[...] = (total + times_rows(d_value, wv_ref[...])).astype(jnp.bfloat16)


def by_head_owner(
    tokens, norm_gain, w_query, w_key, w_value, w_out, w_shorten, first_key, d_faces
):
    tok_rows, model_width = tokens.shape
    face_rows = tok_rows // 9
    width = w_query.shape[1]
    heads = width // HEAD
    seq_count, mp_count = lax.axis_size("seq"), lax.axis_size("mp")
    share = face_rows // mp_count
    halves = 16 // share
    chunk = w_shorten.shape[0] // halves
    padded = -(-chunk // 128) * 128
    tok_total = tok_rows * seq_count
    faces_total = face_rows * seq_count
    bf16, f32 = jnp.bfloat16, jnp.float32

    wide = -(-face_rows // 128) * 128
    bounds = jnp.broadcast_to(jnp.pad(first_key, (0, wide - face_rows))[None], (8, wide))
    all_d_faces, all_bounds = exchange(
        1, [(d_faces, "seq", "same"), (bounds, "seq", "same")]
    )
    low = jnp.repeat(all_bounds[:, 0, :face_rows].reshape(faces_total), 9)[None]

    shorten = jnp.pad(
        w_shorten.reshape(halves, chunk, -1), ((0, 0), (0, padded - chunk), (0, 0))
    )
    by_share = all_d_faces.reshape(seq_count, mp_count, share, -1).transpose(1, 0, 2, 3)
    by_share = by_share.reshape(faces_total, -1)
    d_partial = [
        times_rows(by_share, shorten[half])
        .astype(bf16)
        .reshape(mp_count, seq_count, share, padded)
        for half in range(halves)
    ]
    d_partial = jnp.concatenate(d_partial, axis=2)
    d_partial = d_partial.reshape(mp_count, seq_count * halves * share, padded)

    half_rows = tok_rows // 2
    kv, packed_query = plain_call(
        prepare_kernel,
        (tokens, norm_gain[None], w_query, w_key, w_value),
        (((heads, tok_rows, LANES), bf16), ((heads, half_rows, LANES), bf16)),
    )
    kv, packed_query, d_chunk = exchange(
        2,
        [
            (kv, "seq", "to_heads"),
            (packed_query, "seq", "to_heads"),
            (d_partial, "mp", "reduce"),
        ],
        heads,
    )
    kv = kv.reshape(tok_total, LANES)
    tile, span = tiling(tok_total)
    flat = ((tok_total, LANES), bf16)
    folded = ((seq_count, half_rows, LANES), bf16)
    moved = (seq_count, halves * share, padded)
    query_flat, att_flat, top, inverse, att_packed, d_chunk = forward(
        3, heads, tile, span, kv, packed_query, low, d_chunk.reshape(moved)
    )
    (projected,) = plain_call(
        functools.partial(project_kernel, mp_count),
        (att_packed, w_out, tokens),
        [((tok_rows, model_width), bf16)],
    )
    d_chunk = d_chunk.reshape(seq_count, halves, share, padded)[..., :chunk]
    d_chunk = d_chunk.transpose(2, 0, 1, 3).reshape(tok_rows // mp_count, model_width)
    d_mixed, mixed = exchange(
        4,
        [
            (d_chunk, "mp", "gather"),
            (projected.reshape(mp_count, *d_chunk.shape), "mp", "reduce"),
        ],
    )
    d_mixed = d_mixed.reshape(tok_rows, model_width)
    (d_att_packed,) = plain_call(
        d_attended_kernel, (d_mixed, w_out), [((heads, half_rows, LANES), bf16)]
    )
    mixed = mixed.reshape(share, seq_count, halves, chunk).transpose(1, 2, 0, 3)
    mixed = jnp.pad(mixed, ((0, 0), (0, 0), (0, 0), (0, padded - chunk))).reshape(moved)
    d_att_packed, mixed = exchange(
        5, [(d_att_packed, "seq", "to_heads"), (mixed, "seq", "all")], heads
    )
    d_query, d_kv = plain_call(
        functools.partial(backward_kernel, heads, tile, span),
        (kv, query_flat, d_att_packed, low, att_flat, top, inverse),
        (folded, flat),
        [pltpu.VMEM(*flat), pltpu.VMEM(*flat), pltpu.VMEM(flat[0], f32)],
    )
    d_query, d_kv, mixed = exchange(
        6,
        [
            (d_query, "seq", "from_heads"),
            (d_kv.reshape(seq_count, tok_rows, LANES), "seq", "from_heads"),
            (mixed, "mp", "gather"),
        ],
        heads,
    )
    (part_normed,) = plain_call(
        d_normed_kernel,
        (d_query, d_kv, w_query, w_key, w_value),
        [((tok_rows, model_width), bf16)],
    )
    mixed = mixed.reshape(mp_count, seq_count, halves, share, padded)
    partial = sum(
        jnp.dot(
            mixed[:, :, half].reshape(faces_total, padded),
            shorten[half],
            preferred_element_type=f32,
        )
        for half in range(halves)
    )
    partial = partial.astype(bf16).reshape(mp_count, seq_count, share, -1)
    partial = partial.transpose(1, 0, 2, 3).reshape(seq_count, face_rows, -1)
    part_normed, partial = exchange(
        7,
        [
            (part_normed.reshape(mp_count, *d_chunk.shape), "mp", "reduce"),
            (partial, "seq", "all"),
        ],
    )
    (d_normed,) = exchange(8, [(part_normed, "mp", "gather")])
    faces = jnp.sum(partial.astype(f32), axis=0).astype(bf16)
    d_normed = d_normed.reshape(tok_rows, model_width).astype(f32)
    x_float = tokens.astype(f32)
    scale_r = lax.rsqrt(jnp.mean(x_float * x_float, axis=-1, keepdims=True) + 1e-05)
    d_tokens = finish(d_normed, x_float, scale_r, d_mixed, norm_gain).astype(bf16)
    return (faces, d_tokens)


def by_window(tokens, norm_gain, w_query, w_key, w_value, w_out, w_shorten, first_key, d_faces):
    tok_rows = tokens.shape[0]
    model_width = tokens.shape[1]
    face_rows = tok_rows // 9
    local_width = w_query.shape[1]
    local_heads = local_width // HEAD
    seq_count = lax.axis_size("seq")
    hops = min(-(-WIN // tok_rows), seq_count - 1)
    levels = hops.bit_length()
    seq_index = lax.axis_index("seq")
    x_float = tokens.astype(jnp.float32)
    scale_r = lax.rsqrt(jnp.mean(x_float * x_float, axis=-1, keepdims=True) + 1e-05)
    normed = (x_float * scale_r * norm_gain).astype(jnp.bfloat16)
    query = jnp.dot(normed, w_query, preferred_element_type=jnp.float32).astype(jnp.bfloat16)
    key = jnp.dot(normed, w_key, preferred_element_type=jnp.float32).astype(jnp.bfloat16)
    value = jnp.dot(normed, w_value, preferred_element_type=jnp.float32).astype(jnp.bfloat16)
    stacked_key = key[None]
    stacked_value = value[None]
    for level in range(levels):
        reach_by = 1 << level
        came_key, came_value = shifted((stacked_key, stacked_value), "seq", reach_by)
        stacked_key = jnp.concatenate([stacked_key, came_key], axis=0)
        stacked_value = jnp.concatenate([stacked_value, came_value], axis=0)
    anchors = seq_index - jnp.arange(hops + 1, dtype=jnp.int32)
    block_count = stacked_key.shape[0]
    key_total = block_count * tok_rows
    pos_q = seq_index * tok_rows + jnp.arange(tok_rows, dtype=jnp.int32)
    pos_k = (anchors[:, None] * tok_rows + jnp.arange(tok_rows, dtype=jnp.int32)[None, :]).reshape(
        key_total
    )
    lower_bound = jnp.repeat(first_key, 9)
    allowed = (
        (pos_k[None, :] >= lower_bound[:, None])
        & (pos_k[None, :] <= pos_q[:, None])
        & (pos_q[:, None] - pos_k[None, :] < WIN)
    )
    query_heads = query.reshape(tok_rows, local_heads, HEAD).transpose(1, 0, 2)
    key_heads = stacked_key.reshape(key_total, local_heads, HEAD).transpose(1, 0, 2)
    value_heads = stacked_value.reshape(key_total, local_heads, HEAD).transpose(1, 0, 2)

    def head_probs(query_head, key_head):
        scores = times_rows(query_head, key_head) * HEAD ** (-0.5)
        scores = jnp.where(allowed, scores, -1e30)
        row_top = jnp.max(scores, axis=-1, keepdims=True)
        raised = jnp.exp(scores - row_top)
        return raised / jnp.sum(raised, axis=-1, keepdims=True)

    def head_forward(operands):
        query_head, key_head, value_head = operands
        probs = head_probs(query_head, key_head)
        return jnp.dot(
            probs.astype(jnp.bfloat16), value_head, preferred_element_type=jnp.float32
        ).astype(jnp.bfloat16)

    att_heads = lax.map(head_forward, (query_heads, key_heads, value_heads))
    attended = att_heads.transpose(1, 0, 2).reshape(tok_rows, local_width)
    projected = jnp.dot(attended, w_out, preferred_element_type=jnp.float32)
    summed = lax.psum(projected.astype(jnp.bfloat16), "mp").astype(jnp.float32)
    mixed = (x_float + summed).astype(jnp.bfloat16)
    mixed_faces = mixed.reshape(face_rows, 9 * model_width)
    full_shorten = lax.all_gather(w_shorten, "seq", axis=0, tiled=True)
    face_sum = jnp.dot(mixed_faces, full_shorten, preferred_element_type=jnp.float32)
    d_partial = times_rows(d_faces, full_shorten)
    faces = face_sum.astype(jnp.bfloat16)
    d_mixed = lax.psum(d_partial, "mp").astype(jnp.bfloat16).reshape(tok_rows, model_width)
    d_attended = times_rows(d_mixed, w_out).astype(jnp.bfloat16)
    d_att_heads = d_attended.reshape(tok_rows, local_heads, HEAD).transpose(1, 0, 2)

    def head_backward(operands):
        query_head, key_head, value_head, d_att_head, att_head = operands
        probs = head_probs(query_head, key_head)
        d_probs = times_rows(d_att_head, value_head)
        row_delta = jnp.sum(d_att_head.astype(jnp.float32) * att_head.astype(jnp.float32), axis=-1)
        d_scores = (probs * (d_probs - row_delta[:, None])).astype(jnp.bfloat16)
        d_query_head = (
            jnp.dot(d_scores, key_head, preferred_element_type=jnp.float32) * HEAD ** (-0.5)
        ).astype(jnp.bfloat16)
        d_key_head = times_cols(d_scores, query_head) * HEAD ** (-0.5)
        d_value_head = times_cols(probs.astype(jnp.bfloat16), d_att_head)
        return (d_query_head, d_key_head, d_value_head)

    d_query_heads, d_key_heads, d_value_heads = lax.map(
        head_backward, (query_heads, key_heads, value_heads, d_att_heads, att_heads)
    )
    d_query = d_query_heads.transpose(1, 0, 2).reshape(tok_rows, local_width)
    d_key_parts = d_key_heads.transpose(1, 0, 2).reshape(block_count, tok_rows, local_width)
    d_value_parts = d_value_heads.transpose(1, 0, 2).reshape(block_count, tok_rows, local_width)
    spare_blocks = (1 << levels) - block_count
    filler = jnp.zeros((spare_blocks, tok_rows, local_width), jnp.float32)
    parts_key = jnp.concatenate([d_key_parts, filler], axis=0)
    parts_value = jnp.concatenate([d_value_parts, filler], axis=0)
    for level in reversed(range(levels)):
        reach_by = 1 << level
        came_key, came_value = shifted(
            (
                shortened(parts_key[reach_by : 2 * reach_by]),
                shortened(parts_value[reach_by : 2 * reach_by]),
            ),
            "seq",
            -reach_by,
        )
        parts_key = parts_key[:reach_by] + came_key
        parts_value = parts_value[:reach_by] + came_value
    acc_key, acc_value = (parts_key[0], parts_value[0])
    d_key = acc_key.astype(jnp.bfloat16)
    d_value = acc_value.astype(jnp.bfloat16)
    part_normed = times_rows(d_query, w_query)
    part_normed = part_normed + times_rows(d_key, w_key)
    part_normed = part_normed + times_rows(d_value, w_value)
    d_normed = lax.psum(part_normed.astype(jnp.bfloat16), "mp").astype(jnp.float32)
    d_tokens = finish(d_normed, x_float, scale_r, d_mixed, norm_gain).astype(jnp.bfloat16)
    return (faces, d_tokens)


def local(*arrays):
    heads = arrays[2].shape[1] // HEAD
    seq_count = lax.axis_size("seq")
    whole_pairs = heads % 2 == 0 and lax.axis_size("mp") == 4
    if heads <= seq_count < 2 * heads and whole_pairs:
        return by_head_owner(*arrays)
    return by_window(*arrays)


def solution(mesh):
    in_specs = (
        P("seq", None),
        P(),
        P(None, "mp"),
        P(None, "mp"),
        P(None, "mp"),
        P("mp", None),
        P("seq", "mp"),
        P("seq"),
        P("seq", "mp"),
    )
    out_specs = (P("seq", "mp"), P("seq", None))
    return jax.shard_map(local, mesh=mesh, in_specs=in_specs, out_specs=out_specs, check_vma=False)
```
